128 devices in a mesh: ctx: 8 (over x, z_hi), resp: 16 (over z_lo, y, core).
Axes of the slice: x: 4, y: 4, z: 4 (z_hi: 2, z_lo: 2; z = z_hi * 2 + z_lo), core: 2. Of those that a mesh axis runs over, the one named last changes fastest.
Arguments:
- prompt_hidden: bfloat16 [8, 1024, 5120], P('ctx', 'resp'), may hold values from -6 to 6
- prompt_base: bfloat16 [8, 1024, 5120], P('ctx', 'resp'), may hold values from -22 to 22
- reply_hidden: bfloat16 [8, 16, 128, 5120], P('ctx', 'resp'), may hold values from -6 to 6
- reply_base: bfloat16 [8, 16, 128, 5120], P('ctx', 'resp'), may hold values from -22 to 22
- reply_lengths: int32 [8, 16], P('ctx', 'resp'), may hold values from 16 to 128, as said below
- adapter_down: bfloat16 [3, 5120, 16], replicated, may hold values from -0.078125 to 0.078125
- query_up_weight: bfloat16 [16, 4096], replicated, may hold values from -0.75 to 0.75
- key_value_up_weight: bfloat16 [2, 16, 512], replicated, may hold values from -0.75 to 0.75
- output_down: bfloat16 [4096, 16], replicated, may hold values from -0.09375 to 0.09375
- output_up: bfloat16 [16, 5120], replicated, may hold values from -0.75 to 0.75
- prompt_grad_out: bfloat16 [8, 1024, 5120], P('ctx', 'resp'), may hold values from -0.125 to 0.125
- prompt_grad_base: bfloat16 [8, 1024, 4096], P('ctx', 'resp'), may hold values from -0.125 to 0.125
- reply_grad_out: bfloat16 [8, 16, 128, 5120], P('ctx', 'resp'), may hold values from -0.125 to 0.125
- reply_grad_base: bfloat16 [8, 16, 128, 4096], P('ctx', 'resp'), may hold values from -0.125 to 0.125
Outputs:
- prompt_context: bfloat16 [8, 1024, 4096], P('ctx', 'resp')
- reply_context: bfloat16 [8, 16, 128, 4096], P('ctx', 'resp')
- grad_adapter_down: float32 [3, 5120, 16], replicated
- grad_query_up: float32 [16, 4096], replicated
- grad_keyvalue_up: float32 [2, 16, 512], replicated
- grad_output_down: float32 [4096, 16], replicated
- grad_output_up: float32 [16, 5120], replicated
The draws below stay inside these ranges and needn't reach their ends.
Inputs may be any that keep to these rules, and one draw needn't show every extreme that they name: `reply_lengths`: in each prompt's group one response has all 128 tokens live.
All inputs are finite; a program needn't handle non-finite values.
Results may differ from the reference program's by a relative error of at most 0.023.
Values may be sent and summed in bfloat16 or wider, within the bound.
No kernel may reach another device: no remote copies, remote signals or barrier semaphores. Data moves between devices by JAX's collectives and lax.ppermute only.
A program may use at most 128 MiB of HBM per device.

```python
import jax
import jax.numpy as jnp
from jax import lax

D = 5120
HEAD_DIM = 128
RANK = 16
Q_WIDTH = 4096
KV_WIDTH = 512
PROMPTS = 8
PROMPT_LEN = 1024
REPLY_LEN = 128
REPLIES = 16


def base_rows(key, lead):
    width = Q_WIDTH + 2 * KV_WIDTH
    first = jax.random.fold_in(key, 0)
    shape = lead + (width,)
    noise = jnp.clip(jax.random.normal(first, shape, jnp.float32), -6.0, 6.0)
    return noise.astype(jnp.bfloat16)


def draw_prompt_base(key, part):
    key = jax.random.fold_in(key, 5)
    return base_rows(key, (PROMPTS, PROMPT_LEN))


def draw_reply_base(key, part):
    key = jax.random.fold_in(key, 7)
    return base_rows(key, (PROMPTS, REPLIES, REPLY_LEN))


def draw_reply_lengths(key, part):
    key = jax.random.fold_in(key, 11)
    first, second = jax.random.split(key)
    drawn = jax.random.randint(first, (PROMPTS, REPLIES), REPLY_LEN // 8, REPLY_LEN + 1)
    chosen = jax.random.randint(second, (PROMPTS, 1), 0, REPLIES)
    return jnp.where(jnp.arange(REPLIES)[None, :] == chosen, REPLY_LEN, drawn).astype(jnp.int32)


def levels(rng, shape, pieces, least, top_value):
    level = 1.0
    for axis_at, shards_of in pieces:
        steps = jax.random.uniform(jax.random.fold_in(jax.random.fold_in(rng, 6), axis_at), (shards_of,), jnp.float32, least / len(pieces), top_value / len(pieces))
        level = level * jnp.repeat(jnp.exp(steps), shape[axis_at] // shards_of).reshape((-1,) + (1,) * (len(shape) - 1 - axis_at))
    return level


def normal_values(own_key, dims, deviation, reach, cuts=(), kind=jnp.bfloat16):
    factor_of = levels(own_key, dims, cuts, -0.22, 0.18) if cuts else 1.0
    values = jax.random.normal(own_key, dims, jnp.float32) * deviation * factor_of
    return jnp.minimum(jnp.maximum(values, -reach), reach).astype(kind)


def setup_inputs(seed: int = 0) -> dict:
    arg_keys = jax.random.split(jax.random.key(seed), 15)
    prompt_hidden = normal_values(arg_keys[0], (PROMPTS, PROMPT_LEN, D), 1.0, 6.0, ((0, 8), (1, 16)))
    prompt_base = draw_prompt_base(jax.random.fold_in(arg_keys[14], 71), 0)
    reply_hidden = normal_values(arg_keys[2], (PROMPTS, REPLIES, REPLY_LEN, D), 1.0, 6.0, ((0, 8), (1, 16)))
    reply_base = draw_reply_base(jax.random.fold_in(arg_keys[14], 71), 0)
    reply_lengths = draw_reply_lengths(jax.random.fold_in(arg_keys[14], 71), 0)
    adapter_down = normal_values(arg_keys[5], (3, D, RANK), D ** -0.5, 0.078125)
    query_up_weight = normal_values(arg_keys[6], (RANK, Q_WIDTH), (4 * RANK) ** -0.5, 0.75)
    key_value_up_weight = normal_values(arg_keys[7], (2, RANK, KV_WIDTH), (4 * RANK) ** -0.5, 0.75)
    output_down = normal_values(arg_keys[8], (Q_WIDTH, RANK), Q_WIDTH ** -0.5, 0.09375)
    output_up = normal_values(arg_keys[9], (RANK, D), (4 * RANK) ** -0.5, 0.75)
    prompt_grad_out = normal_values(arg_keys[10], (PROMPTS, PROMPT_LEN, D), 0.02, 0.125, ((0, 8), (1, 16)))
    prompt_grad_base = normal_values(arg_keys[11], (PROMPTS, PROMPT_LEN, Q_WIDTH), 0.02, 0.125, ((0, 8), (1, 16)))
    reply_grad_out = normal_values(arg_keys[12], (PROMPTS, REPLIES, REPLY_LEN, D), 0.02, 0.125, ((0, 8), (1, 16)))
    reply_grad_base = normal_values(arg_keys[13], (PROMPTS, REPLIES, REPLY_LEN, Q_WIDTH), 0.02, 0.125, ((0, 8), (1, 16)))
    return dict(prompt_hidden=prompt_hidden, prompt_base=prompt_base, reply_hidden=reply_hidden, reply_base=reply_base, reply_lengths=reply_lengths, adapter_down=adapter_down, query_up_weight=query_up_weight, key_value_up_weight=key_value_up_weight, output_down=output_down, output_up=output_up, prompt_grad_out=prompt_grad_out, prompt_grad_base=prompt_grad_base, reply_grad_out=reply_grad_out, reply_grad_base=reply_grad_base)


ADAPTER_SCALE = 2.0
ROPE_BASE = 1000000.0
HIGHEST_ACCURACY = lax.Precision.HIGHEST

def apply_rotary(values, token_positions, sign):
    count = values.shape[0]
    heads = values.shape[1] // HEAD_DIM
    middle = HEAD_DIM // 2
    rates = ROPE_BASE ** (-(jnp.arange(middle, dtype=jnp.float32) * (2.0 / HEAD_DIM)))
    angle = token_positions.astype(jnp.float32)[:, None] * rates[None, :]
    cosine = jnp.cos(angle)
    sine = jnp.sin(angle) * sign
    cosine = jnp.concatenate([cosine, cosine], axis=1)[:, None, :]
    sine = jnp.concatenate([sine, sine], axis=1)[:, None, :]
    shaped = values.reshape(count, heads, HEAD_DIM)
    turned = jnp.concatenate([-shaped[:, :, middle:], shaped[:, :, :middle]], axis=2)
    return (shaped * cosine + turned * sine).reshape(count, heads * HEAD_DIM)

def project(hidden_input, base, token_positions, adapter_down, query_up_weight, key_value_up_weight):
    width_q = query_up_weight.shape[1]
    width_kv = key_value_up_weight.shape[2]
    low_rank_query = jnp.dot(hidden_input, adapter_down[0], preferred_element_type=jnp.float32).astype(jnp.bfloat16)
    low_rank_key = jnp.dot(hidden_input, adapter_down[1], preferred_element_type=jnp.float32).astype(jnp.bfloat16)
    low_rank_value = jnp.dot(hidden_input, adapter_down[2], preferred_element_type=jnp.float32).astype(jnp.bfloat16)
    frozen_query_weight = base[:, :width_q].astype(jnp.float32)
    frozen_key_weight = base[:, width_q:width_q + width_kv].astype(jnp.float32)
    frozen_value_weight = base[:, width_q + width_kv:].astype(jnp.float32)
    query_vectors = apply_rotary(frozen_query_weight + ADAPTER_SCALE * jnp.dot(low_rank_query, query_up_weight, preferred_element_type=jnp.float32), token_positions, 1.0).astype(jnp.bfloat16)
    key_matrix_rows = apply_rotary(frozen_key_weight + ADAPTER_SCALE * jnp.dot(low_rank_key, key_value_up_weight[0], preferred_element_type=jnp.float32), token_positions, 1.0).astype(jnp.bfloat16)
    value_matrix_rows = (frozen_value_weight + ADAPTER_SCALE * jnp.dot(low_rank_value, key_value_up_weight[1], preferred_element_type=jnp.float32)).astype(jnp.bfloat16)
    return (query_vectors, key_matrix_rows, value_matrix_rows, (low_rank_query, low_rank_key, low_rank_value))

def output_back(grad_out, grad_base, live, output_down, output_up):
    incoming_gradient = jnp.where(live[:, None], grad_out, jnp.zeros_like(grad_out))
    incoming_base_gradient = jnp.where(live[:, None], grad_base, jnp.zeros_like(grad_base))
    reduced_product = jnp.dot(incoming_gradient, output_up.T, preferred_element_type=jnp.float32)
    broadcast_heads = jnp.dot(reduced_product, output_down.astype(jnp.float32).T, precision=HIGHEST_ACCURACY)
    backward_step = (incoming_base_gradient.astype(jnp.float32) + ADAPTER_SCALE * broadcast_heads).astype(jnp.bfloat16)
    return (incoming_gradient, reduced_product, backward_step)

def attend(query_vectors, backward_step, keys, values, allowed, live):
    rows = query_vectors.shape[0]
    count = keys.shape[0]
    groups = keys.shape[1] // HEAD_DIM
    share = query_vectors.shape[1] // keys.shape[1]
    scale = HEAD_DIM ** (-0.5)

    def split_heads(array, width):
        return array.reshape(array.shape[0], groups, width).transpose(1, 0, 2)

    def one_group(inputs):
        query_block, push_block, key_block, value_block = inputs
        query_heads = query_block.reshape(rows, share, HEAD_DIM).astype(jnp.float32)
        push_heads = push_block.reshape(rows, share, HEAD_DIM).astype(jnp.float32)
        key_head = key_block.astype(jnp.float32)
        value_head = value_block.astype(jnp.float32)
        scores = jnp.einsum('rgd,kd->rgk', query_heads, key_head, precision=HIGHEST_ACCURACY) * scale
        scores = jnp.where(allowed[:, None, :], scores, -jnp.inf)
        top = lax.optimization_barrier(jnp.max(scores, axis=2, keepdims=True))
        weight = jnp.exp(scores - top)
        prob = weight / lax.optimization_barrier(jnp.sum(weight, axis=2, keepdims=True))
        chosen = lax.optimization_barrier(prob.astype(jnp.bfloat16)).astype(jnp.float32)
        mixed = jnp.einsum('rgk,kd->rgd', chosen, value_head, precision=HIGHEST_ACCURACY).astype(jnp.bfloat16)
        mixed = jnp.where(live[:, None, None], mixed, jnp.zeros_like(mixed))
        delta = lax.optimization_barrier(jnp.sum(mixed.astype(jnp.float32) * push_heads, axis=2, keepdims=True))
        dprob = jnp.einsum('rgd,kd->rgk', push_heads, value_head, precision=HIGHEST_ACCURACY)
        dscore = lax.optimization_barrier((prob * (dprob - delta)).astype(jnp.bfloat16)).astype(jnp.float32)
        dquery = jnp.einsum('rgk,kd->rgd', dscore, key_head, precision=HIGHEST_ACCURACY) * scale
        dkey = jnp.einsum('rgk,rgd->kd', dscore, query_heads, precision=HIGHEST_ACCURACY) * scale
        dvalue = jnp.einsum('rgk,rgd->kd', chosen, push_heads, precision=HIGHEST_ACCURACY)
        return (mixed.reshape(rows, share * HEAD_DIM), dquery.reshape(rows, share * HEAD_DIM), dkey, dvalue)
    stacked = (split_heads(query_vectors, share * HEAD_DIM), split_heads(backward_step, share * HEAD_DIM), split_heads(keys, HEAD_DIM), split_heads(values, HEAD_DIM))
    attended_output, dquery, dkey, dvalue = lax.map(one_group, stacked)

    def merge_heads(array, length):
        return array.transpose(1, 0, 2).reshape(length, -1)
    return (merge_heads(attended_output, rows), merge_heads(dquery, rows), merge_heads(dkey, count), merge_heads(dvalue, count))

def fold_back(unrotated_input, adapter_out):
    return jnp.dot(unrotated_input, adapter_out.astype(jnp.float32).T, precision=HIGHEST_ACCURACY)

def low_grad(low_rank_state, unrotated_input):
    return ADAPTER_SCALE * jnp.einsum('sg,su->gu', low_rank_state.astype(jnp.float32), unrotated_input, precision=HIGHEST_ACCURACY)

def input_grads(hidden_input, fold_q, fold_k, fold_v):
    folded_gradients = jnp.stack([fold_q, fold_k, fold_v])
    return ADAPTER_SCALE * jnp.einsum('gq,xgs->xqs', hidden_input.astype(jnp.float32), folded_gradients, precision=HIGHEST_ACCURACY)

def output_grads(attended_output, reduced_product, incoming_gradient, output_down):
    down_weight_gradient = ADAPTER_SCALE * jnp.einsum('ym,yp->mp', attended_output.astype(jnp.float32), reduced_product, precision=HIGHEST_ACCURACY)
    raised_product = jnp.dot(attended_output, output_down, preferred_element_type=jnp.float32)
    up_weight_gradient = ADAPTER_SCALE * jnp.einsum('cw,cl->wl', raised_product, incoming_gradient.astype(jnp.float32), precision=HIGHEST_ACCURACY)
    return (down_weight_gradient, up_weight_gradient)

def one_prompt(prompt_hidden, prompt_base, reply_hidden, reply_base, reply_lengths, adapter_down, query_up_weight, key_value_up_weight, output_down, output_up, prompt_grad_out, prompt_grad_base, reply_grad_out, reply_grad_base):
    all_places = jnp.arange(PROMPT_LEN, dtype=jnp.int32)
    every = jnp.ones((PROMPT_LEN,), dtype=bool)
    prompt_query, prompt_key, prompt_value, prompt_low = project(prompt_hidden, prompt_base, all_places, adapter_down, query_up_weight, key_value_up_weight)
    prompt_cot, prompt_lowered, prompt_push = output_back(prompt_grad_out, prompt_grad_base, every, output_down, output_up)
    block = min(512, PROMPT_LEN)
    blocks = PROMPT_LEN // block
    zero_keys = jnp.zeros((PROMPT_LEN, KV_WIDTH), jnp.float32)

    def prompt_step(carry, inputs):
        query_vectors, backward_step, token_positions = inputs
        allowed = all_places[None, :] <= token_positions[:, None]
        attended_output, dquery, dkey, dvalue = attend(query_vectors, backward_step, prompt_key, prompt_value, allowed, jnp.ones((block,), dtype=bool))
        return ((carry[0] + dkey, carry[1] + dvalue), (attended_output, dquery))
    (prompt_dkey, prompt_dvalue), (prompt_context, prompt_dquery) = lax.scan(prompt_step, (zero_keys, zero_keys), (prompt_query.reshape(blocks, block, Q_WIDTH), prompt_push.reshape(blocks, block, Q_WIDTH), all_places.reshape(blocks, block)))
    prompt_context = prompt_context.reshape(PROMPT_LEN, Q_WIDTH)
    prompt_dquery = prompt_dquery.reshape(PROMPT_LEN, Q_WIDTH)
    token_index = jnp.arange(REPLY_LEN, dtype=jnp.int32)
    reply_places = PROMPT_LEN + token_index
    reply_allowed = jnp.concatenate([jnp.ones((REPLY_LEN, PROMPT_LEN), dtype=bool), token_index[None, :] <= token_index[:, None]], axis=1)

    def reply_step(carry, inputs):
        hidden_input, base, grad_out, grad_base, length = inputs
        live = token_index < length
        query_vectors, key_matrix_rows, value_matrix_rows, low_rank_state = project(hidden_input, base, reply_places, adapter_down, query_up_weight, key_value_up_weight)
        incoming_gradient, reduced_product, backward_step = output_back(grad_out, grad_base, live, output_down, output_up)
        attended_output, dquery, dkey, dvalue = attend(query_vectors, backward_step, jnp.concatenate([prompt_key, key_matrix_rows], axis=0), jnp.concatenate([prompt_value, value_matrix_rows], axis=0), reply_allowed, live)
        raw_q = apply_rotary(dquery, reply_places, -1.0)
        raw_k = apply_rotary(dkey[PROMPT_LEN:], reply_places, -1.0)
        raw_v = dvalue[PROMPT_LEN:]
        down = input_grads(hidden_input, fold_back(raw_q, query_up_weight), fold_back(raw_k, key_value_up_weight[0]), fold_back(raw_v, key_value_up_weight[1]))
        pair = jnp.stack([low_grad(low_rank_state[1], raw_k), low_grad(low_rank_state[2], raw_v)])
        down_weight_gradient, up_weight_gradient = output_grads(attended_output, reduced_product, incoming_gradient, output_down)
        fresh = (carry[0] + dkey[:PROMPT_LEN], carry[1] + dvalue[:PROMPT_LEN], carry[2] + down, carry[3] + low_grad(low_rank_state[0], raw_q), carry[4] + pair, carry[5] + down_weight_gradient, carry[6] + up_weight_gradient)
        return (fresh, attended_output)
    start = (zero_keys, zero_keys, jnp.zeros((3, D, RANK), jnp.float32), jnp.zeros((RANK, Q_WIDTH), jnp.float32), jnp.zeros((2, RANK, KV_WIDTH), jnp.float32), jnp.zeros((Q_WIDTH, RANK), jnp.float32), jnp.zeros((RANK, D), jnp.float32))
    totals, reply_context = lax.scan(reply_step, start, (reply_hidden, reply_base, reply_grad_out, reply_grad_base, reply_lengths))
    total_dkey = prompt_dkey + totals[0]
    total_dvalue = prompt_dvalue + totals[1]
    raw_key = apply_rotary(total_dkey, all_places, -1.0)
    raw_query = apply_rotary(prompt_dquery, all_places, -1.0)
    grad_adapter_down = totals[2] + input_grads(prompt_hidden, fold_back(raw_query, query_up_weight), fold_back(raw_key, key_value_up_weight[0]), fold_back(total_dvalue, key_value_up_weight[1]))
    grad_query_up = totals[3] + low_grad(prompt_low[0], raw_query)
    grad_keyvalue_up = totals[4] + jnp.stack([low_grad(prompt_low[1], raw_key), low_grad(prompt_low[2], total_dvalue)])
    down_weight_gradient, up_weight_gradient = output_grads(prompt_context, prompt_lowered, prompt_cot, output_down)
    return (prompt_context, reply_context, grad_adapter_down, grad_query_up, grad_keyvalue_up, totals[5] + down_weight_gradient, totals[6] + up_weight_gradient)

def reference(prompt_hidden, prompt_base, reply_hidden, reply_base, reply_lengths, adapter_down, query_up_weight, key_value_up_weight, output_down, output_up, prompt_grad_out, prompt_grad_base, reply_grad_out, reply_grad_base):

    def group_step(carry, inputs):
        p_hidden, p_base, r_hidden, r_base, r_lengths, p_out, p_grad_base, r_out, r_grad_base = inputs
        result = one_prompt(p_hidden, p_base, r_hidden, r_base, r_lengths, adapter_down, query_up_weight, key_value_up_weight, output_down, output_up, p_out, p_grad_base, r_out, r_grad_base)
        fresh = (carry[0] + result[2], carry[1] + result[3], carry[2] + result[4], carry[3] + result[5], carry[4] + result[6])
        return (fresh, (result[0], result[1]))
    start = (jnp.zeros((3, D, RANK), jnp.float32), jnp.zeros((RANK, Q_WIDTH), jnp.float32), jnp.zeros((2, RANK, KV_WIDTH), jnp.float32), jnp.zeros((Q_WIDTH, RANK), jnp.float32), jnp.zeros((RANK, D), jnp.float32))
    totals, contexts = lax.scan(group_step, start, (prompt_hidden, prompt_base, reply_hidden, reply_base, reply_lengths, prompt_grad_out, prompt_grad_base, reply_grad_out, reply_grad_base))
    return (contexts[0], contexts[1], totals[0], totals[1], totals[2], totals[3], totals[4])
```

```python
import functools

import jax
import jax.numpy as jnp
import numpy as np
from jax import lax
from jax.experimental import pallas as pl
from jax.experimental.pallas import tpu as pltpu
from jax.sharding import PartitionSpec as P

HEAD_DIM = 128
HALF = 64
RANK = 16
ROPE_BASE = 1000000.0
LOG2E = 1.4426950408889634
F32 = jnp.float32
BF16 = jnp.bfloat16
BOTH = ("ctx", "resp")
VMEM_LIMIT = 56 * 1024 * 1024

NN = (((1,), (0,)), ((), ()))
NT = (((1,), (1,)), ((), ()))
TN = (((0,), (0,)), ((), ()))


def mm(a, b, dims=NN):
    return lax.dot_general(a, b, dims, preferred_element_type=F32)


def rope_tables(count):
    rates = ROPE_BASE ** (-(np.arange(HALF, dtype=np.float64) * (2.0 / HEAD_DIM)))
    angle = np.arange(count, dtype=np.float64)[:, None] * rates[None, :]
    return np.cos(angle), np.sin(angle)


def rope(x, cos, sin):
    return x * cos + pltpu.roll(x, HALF, 1) * sin


def unrope(x, cos, sin):
    return x * cos - pltpu.roll(x, HALF, 1) * sin


def params(flops=0, nbytes=0):
    return dict(
        compiler_params=pltpu.CompilerParams(vmem_limit_bytes=VMEM_LIMIT),
        cost_estimate=pl.CostEstimate(flops=flops, bytes_accessed=nbytes, transcendentals=0),
    )


def kv_rows(hidden, base, down, kv_up, cos, sin):
    kv_width = kv_up.shape[2]
    low = mm(hidden, down, NT).astype(BF16)
    zero = jnp.zeros((RANK, kv_width), BF16)
    k_lift = jnp.concatenate([zero, kv_up[0], zero], axis=0)
    v_lift = jnp.concatenate([zero, zero, kv_up[1]], axis=0)
    key = base[:, :kv_width].astype(F32) + 2.0 * mm(low, k_lift)
    value = base[:, kv_width:].astype(F32) + 2.0 * mm(low, v_lift)
    heads = [
        rope(key[:, h : h + HEAD_DIM], cos, sin).astype(BF16)
        for h in range(0, kv_width, HEAD_DIM)
    ]
    return low, jnp.concatenate(heads, axis=1), value.astype(BF16)


def pad_low(low):
    return jnp.concatenate([low, jnp.zeros((low.shape[0], HEAD_DIM - 3 * RANK), BF16)], axis=1)


def front_kernel(spot, hidden, base, down, kv_up, cos, sin, out):
    low, key, value = kv_rows(hidden[0], base[0], down[...], kv_up[...], cos[...], sin[...])
    out[...] = jnp.concatenate([key, value, pad_low(low)], axis=1)


def prep_kernel(
    spot, lengths, p_low, p_base, p_out, p_gbase, r_hidden, r_base, r_kvbase, r_out, r_gbase,
    down, q_up, kv_up, out_down, out_up, p_cos, p_sin, r_cos, r_sin,
    query, push, r_kv, low_t, lowered_t,
):
    pr = p_low.shape[0]
    rl = r_hidden.shape[2]
    q_width = q_up.shape[1]
    r_low, r_key, r_value = kv_rows(
        r_hidden[0, 0], r_kvbase[0, 0], down[...], kv_up[...], r_cos[...], r_sin[...]
    )
    r_low = pad_low(r_low)
    r_kv[...] = jnp.concatenate([r_key, r_value, r_low], axis=1)
    lows = (p_low[...], r_low)
    for low, rows in ((lows[0], pl.ds(0, pr)), (lows[1], pl.ds(pr, rl))):
        low_t[:, rows] = jnp.transpose(low.astype(F32))[: 3 * RANK].astype(BF16)
    live = lax.broadcasted_iota(jnp.int32, (rl, HEAD_DIM), 0) < lengths[0, 0]
    p_lowered = mm(p_out[0], out_up[...], NT)
    r_lowered = mm(r_out[0, 0], out_up[...], NT)
    r_lowered = jnp.where(live[:, :RANK], r_lowered, 0.0)
    split = []
    for lowered, at, n in ((p_lowered, 0, pr), (r_lowered, pr, rl)):
        high = lowered.astype(BF16)
        rest = (lowered - high.astype(F32)).astype(BF16)
        zero = jnp.zeros((n, HEAD_DIM - 2 * RANK), BF16)
        both = jnp.concatenate([high, rest, zero], axis=1)
        split.append(both)
        lowered_t[:, pl.ds(at, n)] = jnp.transpose(both.astype(F32))[: 2 * RANK].astype(BF16)
    for c in range(0, q_width, 1024):
        cols = slice(c, c + 1024)
        q_lift = jnp.concatenate(
            [q_up[:, cols], jnp.zeros((HEAD_DIM - RANK, 1024), BF16)], axis=0
        )
        o_lift = jnp.concatenate(
            [out_down[:, cols], out_down[:, cols], jnp.zeros((HEAD_DIM - 2 * RANK, 1024), BF16)],
            axis=0,
        )
        for i, (base, gbase, cos, sin, at, n) in enumerate(
            (
                (p_base[0, :, cols], p_gbase[0, :, cols], p_cos, p_sin, 0, pr),
                (r_base[0, 0, :, cols], r_gbase[0, 0, :, cols], r_cos, r_sin, pr, rl),
            )
        ):
            q = base.astype(F32) + 2.0 * mm(lows[i], q_lift)
            for h in range(0, 1024, HEAD_DIM):
                query[at : at + n, c + h : c + h + HEAD_DIM] = rope(
                    q[:, h : h + HEAD_DIM], cos[...], sin[...]
                ).astype(BF16)
            up = gbase.astype(F32) + 2.0 * mm(split[i], o_lift)
            if i == 1:
                up = jnp.where(live[:, :1], up, 0.0)
            push[at : at + n, c : c + 1024] = up.astype(BF16)


def attend_kernel(
    spot, lengths, query, push, key, value, low, r_key, r_value, r_low, low_t, lowered_t,
    q_up, kv_up, out_down, p_cos, p_sin, r_cos, r_sin, cos_t, sin_t,
    p_context, r_context, grad_q, grad_kv, grad_od, fold_q, lifted, fold_send, fold_reply,
    dk_t, dv_t, raw_q, mixed, keys, values, bias, fold_k, fold_v,
):
    g = pl.program_id(0)
    last = pl.num_programs(0) - 1
    pr = p_context.shape[1]
    rl = r_context.shape[2]
    prompt = key.shape[0]
    scale = HEAD_DIM ** (-0.5)
    step = scale * LOG2E
    share = query.shape[1] // HEAD_DIM
    block = 256

    @pl.when(g == 0)
    def _():
        row = lax.broadcasted_iota(jnp.int32, (pr, prompt), 0) + spot[0] * pr
        col = lax.broadcasted_iota(jnp.int32, (pr, prompt), 1)
        bias[...] = jnp.where(col <= row, 0.0, -jnp.inf)
        fold_q[...] = jnp.zeros_like(fold_q)
        lifted[...] = jnp.zeros_like(lifted)
        fold_k[...] = jnp.zeros_like(fold_k)
        fold_v[...] = jnp.zeros_like(fold_v)
        values[:, HEAD_DIM:] = jnp.ones((prompt + rl, HEAD_DIM), BF16)

    keys[:prompt, :] = key[...]
    keys[prompt:, :] = r_key[...]
    values[:prompt, :HEAD_DIM] = value[...]
    values[prompt:, :HEAD_DIM] = r_value[...]
    dk_t[...] = jnp.zeros_like(dk_t)
    dv_t[...] = jnp.zeros_like(dv_t)

    def one_block(rows, n, at, heads, mask, keep, cos, sin, count):
        def stack(ref):
            return jnp.concatenate(
                [ref[pl.ds(at, n), pl.ds(pl.multiple_of(h * HEAD_DIM, HEAD_DIM), HEAD_DIM)] for h in heads],
                axis=0,
            )

        q = stack(query)
        p = stack(push)
        k = keys[:count, :]
        v = values[:count, :HEAD_DIM]
        score = mask(mm(q, k, NT))
        top = jnp.max(score, axis=1, keepdims=True) * step
        weight = jnp.exp2(score * step - top).astype(BF16)
        summed = mm(weight, values[:count, :])
        share_of = 1.0 / summed[:, HEAD_DIM:]
        context = (summed[:, :HEAD_DIM] * share_of).astype(BF16)
        context = keep(context)
        delta = jnp.sum(context.astype(F32) * p.astype(F32), axis=1, keepdims=True)
        dprob = mm(p, v, NT)
        dscore = (weight.astype(F32) * (dprob - delta)).astype(BF16)
        inverse = share_of * scale
        dq = mm(dscore, k) * inverse
        dk_t[:, :count] += mm((q.astype(F32) * inverse).astype(BF16), dscore, TN)
        dv_t[:, :count] += mm((p.astype(F32) * share_of).astype(BF16), weight, TN)
        for i, h in enumerate(heads):
            part = slice(i * n, (i + 1) * n)
            cols = pl.ds(pl.multiple_of(h * HEAD_DIM, HEAD_DIM), HEAD_DIM)
            raw_q[pl.ds(at, n), cols] = unrope(dq[part], cos[...], sin[...]).astype(BF16)
            mixed[pl.ds(at, n), cols] = context[part]

    p_heads = block // pr
    r_heads = block // rl

    def p_mask(score):
        seen = bias[...]
        return jnp.concatenate(
            [score[i * pr : (i + 1) * pr] + seen for i in range(p_heads)], axis=0
        )

    for b in range(share // p_heads):
        one_block(
            block, pr, 0, [b * p_heads + i for i in range(p_heads)], p_mask,
            lambda c: c, p_cos, p_sin, prompt,
        )

    r_row = lax.broadcasted_iota(jnp.int32, (rl, rl), 0)
    r_col = lax.broadcasted_iota(jnp.int32, (rl, rl), 1)
    r_seen = jnp.concatenate([r_col <= r_row] * r_heads, axis=0)
    live = jnp.concatenate([r_row < lengths[0, 0]] * r_heads, axis=0)

    def r_mask(score):
        own = jnp.where(r_seen, score[:, prompt:], -jnp.inf)
        return jnp.concatenate([score[:, :prompt], own], axis=1)

    for b in range(share // r_heads):
        one_block(
            block, rl, pr, [b * r_heads + i for i in range(r_heads)], r_mask,
            lambda c: jnp.where(live, c, jnp.zeros_like(c)), r_cos, r_sin, prompt + rl,
        )

    context = mixed[...]
    p_context[0] = mixed[:pr, :]
    r_context[0, 0] = mixed[pr:, :]
    raw = raw_q[...]
    grad_q[...] = (2.0 * mm(low_t[:RANK, :], raw)).astype(BF16)
    both = mm(lowered_t[...], context)
    grad_od[...] = (2.0 * (both[:RANK] + both[RANK:])).astype(BF16)
    fold_q[...] += mm(q_up[...], raw, NT)
    lifted[...] += mm(out_down[...], context, NT)
    upper, lower = dk_t[:HALF, :], dk_t[HALF:, :]
    cos, sin = cos_t[...], sin_t[...]
    raw_k = jnp.concatenate(
        [(upper * cos + lower * sin).astype(BF16), (lower * cos - upper * sin).astype(BF16)], axis=0
    )
    raw_v = dv_t[...].astype(BF16)
    fold_k[...] += mm(kv_up[0], raw_k)
    fold_v[...] += mm(kv_up[1], raw_v)
    gk = mm(raw_k[:, :prompt], low[...]) + mm(raw_k[:, prompt:], r_low[...])
    gv = mm(raw_v[:, :prompt], low[...]) + mm(raw_v[:, prompt:], r_low[...])
    gk, gv = jnp.transpose(gk), jnp.transpose(gv)
    grad_kv[...] = (
        2.0 * jnp.concatenate([gk[RANK : 2 * RANK], gv[2 * RANK : 3 * RANK]], axis=0)
    ).astype(BF16)

    @pl.when(g == last)
    def _():
        fk, fv = fold_k[...], fold_v[...]
        for r in range(prompt // pr):
            cols = slice(r * pr, (r + 1) * pr)
            fold_send[r] = jnp.concatenate([fk[:, cols], fv[:, cols]], axis=1).astype(BF16)
        fold_reply[...] = jnp.concatenate([fk[:, prompt:], fv[:, prompt:]], axis=0).astype(BF16)


def grads_kernel(
    fold_q, lifted, fold_reply, fold_recv, p_hidden, r_hidden, p_out, r_out, grad_down, grad_up
):
    pr = p_hidden.shape[1]
    fq = fold_q[...].astype(BF16)
    up = lifted[...].astype(BF16)
    own = jnp.sum(fold_recv[...].astype(F32), axis=0).astype(BF16)
    fp = jnp.concatenate([fq[:, :pr], own[:, :pr], own[:, pr:]], axis=0)
    fr = jnp.concatenate([fq[:, pr:], fold_reply[...]], axis=0)
    d = p_hidden.shape[2]
    down = 2.0 * (mm(fp, p_hidden[0]) + mm(fr, r_hidden[0, 0]))
    grad_down[...] = down.astype(BF16)
    grad_up[...] = (2.0 * (mm(up[:, :pr], p_out[0]) + mm(up[:, pr:], r_out[0, 0]))).astype(BF16)


def whole(shape):
    return pl.BlockSpec(shape, lambda *_: (0,) * len(shape))


def per_device(
    prompt_hidden,
    prompt_base,
    reply_hidden,
    reply_base,
    reply_lengths,
    adapter_down,
    query_up_weight,
    key_value_up_weight,
    output_down,
    output_up,
    prompt_grad_out,
    prompt_grad_base,
    reply_grad_out,
    reply_grad_base,
):
    group = lax.axis_size("resp")
    everyone = group * lax.axis_size("ctx")
    pr = prompt_hidden.shape[1]
    rl = reply_hidden.shape[2]
    d = prompt_hidden.shape[2]
    prompt = pr * group
    q_width = query_up_weight.shape[1]
    kv_width = key_value_up_weight.shape[2]
    heads = kv_width // HEAD_DIM
    qb = q_width // heads
    rows = pr + rl
    wide = 2 * kv_width + HEAD_DIM
    low_at = 2 * kv_width // HEAD_DIM

    spot = lax.axis_index("resp").astype(jnp.int32)[None]
    down = jnp.transpose(adapter_down, (0, 2, 1)).reshape(3 * RANK, d)
    out_down = jnp.transpose(output_down)
    cos, sin = rope_tables(prompt + rl)
    cos_rows = jnp.asarray(np.concatenate([cos, cos], axis=1), F32)
    sin_rows = jnp.asarray(np.concatenate([-sin, sin], axis=1), F32)
    cos_t = jnp.asarray(cos.T, F32)
    sin_t = jnp.asarray(sin.T, F32)
    p_table = pl.BlockSpec((pr, HEAD_DIM), lambda i, s: (s[0], 0))
    r_table = pl.BlockSpec((rl, HEAD_DIM), lambda i, s: (prompt // rl, 0))

    own_kv = pl.pallas_call(
        front_kernel,
        grid_spec=pltpu.PrefetchScalarGridSpec(
            num_scalar_prefetch=1,
            grid=(1,),
            in_specs=[
                whole((1, pr, d)),
                pl.BlockSpec((1, pr, 2 * kv_width), lambda i, s: (0, 0, q_width // (2 * kv_width))),
                whole((3 * RANK, d)),
                whole((2, RANK, kv_width)),
                p_table,
                p_table,
            ],
            out_specs=whole((pr, wide)),
        ),
        out_shape=jax.ShapeDtypeStruct((pr, wide), BF16),
        name="front",
        **params(2 * pr * d * 48, 2_000_000),
    )(spot, prompt_hidden, prompt_base, down, key_value_up_weight, cos_rows, sin_rows)

    all_kv = lax.all_gather(own_kv, "resp", axis=0, tiled=True)

    query, push, reply_kv, low_t, lowered_t = pl.pallas_call(
        prep_kernel,
        grid_spec=pltpu.PrefetchScalarGridSpec(
            num_scalar_prefetch=1,
            grid=(1,),
            in_specs=[
                pl.BlockSpec(memory_space=pltpu.SMEM),
                pl.BlockSpec((pr, HEAD_DIM), lambda i, s: (0, low_at)),
                pl.BlockSpec((1, pr, q_width), lambda i, s: (0, 0, 0)),
                whole((1, pr, d)),
                whole((1, pr, q_width)),
                whole((1, 1, rl, d)),
                pl.BlockSpec((1, 1, rl, q_width), lambda i, s: (0, 0, 0, 0)),
                pl.BlockSpec(
                    (1, 1, rl, 2 * kv_width), lambda i, s: (0, 0, 0, q_width // (2 * kv_width))
                ),
                whole((1, 1, rl, d)),
                whole((1, 1, rl, q_width)),
                whole((3 * RANK, d)),
                whole((RANK, q_width)),
                whole((2, RANK, kv_width)),
                whole((RANK, q_width)),
                whole((RANK, d)),
                p_table,
                p_table,
                r_table,
                r_table,
            ],
            out_specs=[
                whole((rows, q_width)),
                whole((rows, q_width)),
                whole((rl, wide)),
                whole((3 * RANK, rows)),
                whole((2 * RANK, rows)),
            ],
        ),
        out_shape=[
            jax.ShapeDtypeStruct((rows, q_width), BF16),
            jax.ShapeDtypeStruct((rows, q_width), BF16),
            jax.ShapeDtypeStruct((rl, wide), BF16),
            jax.ShapeDtypeStruct((3 * RANK, rows), BF16),
            jax.ShapeDtypeStruct((2 * RANK, rows), BF16),
        ],
        name="prep",
        **params(4 * rows * d * 48, 12_000_000),
    )(
        spot, reply_lengths, own_kv, prompt_base, prompt_grad_out, prompt_grad_base, reply_hidden,
        reply_base, reply_base, reply_grad_out, reply_grad_base, down, query_up_weight,
        key_value_up_weight, out_down, output_up, cos_rows, sin_rows, cos_rows, sin_rows,
    )

    def head_cols(n, width, shift=0):
        return pl.BlockSpec((n, width), lambda i, s: (0, i + shift))

    (
        p_context, r_context, grad_q, grad_kv, grad_od, fold_q, lifted, fold_send, fold_reply,
    ) = pl.pallas_call(
        attend_kernel,
        grid_spec=pltpu.PrefetchScalarGridSpec(
            num_scalar_prefetch=1,
            grid=(heads,),
            in_specs=[
                pl.BlockSpec(memory_space=pltpu.SMEM),
                head_cols(rows, qb),
                head_cols(rows, qb),
                head_cols(prompt, HEAD_DIM),
                head_cols(prompt, HEAD_DIM, heads),
                pl.BlockSpec((prompt, HEAD_DIM), lambda i, s: (0, low_at)),
                head_cols(rl, HEAD_DIM),
                head_cols(rl, HEAD_DIM, heads),
                pl.BlockSpec((rl, HEAD_DIM), lambda i, s: (0, low_at)),
                whole((3 * RANK, rows)),
                whole((2 * RANK, rows)),
                head_cols(RANK, qb),
                pl.BlockSpec((2, RANK, HEAD_DIM), lambda i, s: (0, 0, i)),
                head_cols(RANK, qb),
                p_table,
                p_table,
                r_table,
                r_table,
                whole((HALF, prompt + rl)),
                whole((HALF, prompt + rl)),
            ],
            out_specs=[
                pl.BlockSpec((1, pr, qb), lambda i, s: (0, 0, i)),
                pl.BlockSpec((1, 1, rl, qb), lambda i, s: (0, 0, 0, i)),
                head_cols(RANK, qb),
                head_cols(2 * RANK, HEAD_DIM),
                head_cols(RANK, qb),
                whole((RANK, rows)),
                whole((RANK, rows)),
                whole((group, RANK, 2 * pr)),
                whole((2 * RANK, rl)),
            ],
            scratch_shapes=[
                pltpu.VMEM((HEAD_DIM, prompt + rl), F32),
                pltpu.VMEM((HEAD_DIM, prompt + rl), F32),
                pltpu.VMEM((rows, qb), BF16),
                pltpu.VMEM((rows, qb), BF16),
                pltpu.VMEM((prompt + rl, HEAD_DIM), BF16),
                pltpu.VMEM((prompt + rl, 2 * HEAD_DIM), BF16),
                pltpu.VMEM((pr, prompt), F32),
                pltpu.VMEM((RANK, prompt + rl), F32),
                pltpu.VMEM((RANK, prompt + rl), F32),
            ],
        ),
        out_shape=[
            jax.ShapeDtypeStruct((1, pr, q_width), BF16),
            jax.ShapeDtypeStruct((1, 1, rl, q_width), BF16),
            jax.ShapeDtypeStruct((RANK, q_width), BF16),
            jax.ShapeDtypeStruct((2 * RANK, kv_width), BF16),
            jax.ShapeDtypeStruct((RANK, q_width), BF16),
            jax.ShapeDtypeStruct((RANK, rows), F32),
            jax.ShapeDtypeStruct((RANK, rows), F32),
            jax.ShapeDtypeStruct((group, RANK, 2 * pr), BF16),
            jax.ShapeDtypeStruct((2 * RANK, rl), BF16),
        ],
        name="attend",
        **params(12 * rows * prompt * q_width, 8_000_000),
    )(
        spot, reply_lengths, query, push, all_kv, all_kv, all_kv, reply_kv, reply_kv, reply_kv,
        low_t, lowered_t, query_up_weight, key_value_up_weight, out_down, cos_rows, sin_rows,
        cos_rows, sin_rows, cos_t, sin_t,
    )

    fold_recv = lax.all_to_all(fold_send, "resp", 0, 0, tiled=True)

    grad_down, grad_up = pl.pallas_call(
        grads_kernel,
        out_shape=[
            jax.ShapeDtypeStruct((3 * RANK, d), BF16),
            jax.ShapeDtypeStruct((RANK, d), BF16),
        ],
        name="grads",
        **params(2 * rows * d * 64, 5_000_000),
    )(
        fold_q, lifted, fold_reply, fold_recv, prompt_hidden, reply_hidden, prompt_grad_out,
        reply_grad_out,
    )

    pieces = (grad_down, grad_up, grad_q, grad_od, grad_kv)
    flat = jnp.concatenate([x.reshape(-1) for x in pieces])
    unit = everyone * 8 * HEAD_DIM
    total = -(-flat.size // unit) * unit
    flat = jnp.concatenate([flat, jnp.zeros((total - flat.size,), BF16)])
    spread = lax.all_to_all(flat.reshape(everyone, -1, HEAD_DIM), BOTH, 0, 0, tiled=True)
    mine = jnp.sum(spread.astype(F32), axis=0).astype(BF16)
    full = lax.all_to_all(
        jnp.broadcast_to(mine[None], spread.shape), BOTH, 0, 0, tiled=True
    ).reshape(-1)
    outs = []
    at = 0
    for x in pieces:
        outs.append(full[at : at + x.size].reshape(x.shape).astype(F32))
        at += x.size
    sum_down, sum_up, sum_q, sum_od, sum_kv = outs
    return (
        p_context,
        r_context,
        jnp.transpose(sum_down.reshape(3, RANK, d), (0, 2, 1)),
        sum_q,
        sum_kv.reshape(2, RANK, kv_width),
        jnp.transpose(sum_od),
        sum_up,
    )


def solution(mesh):
    return jax.shard_map(
        per_device,
        mesh=mesh,
        in_specs=(
            P("ctx", "resp", None),
            P("ctx", "resp", None),
            P("ctx", "resp", None, None),
            P("ctx", "resp", None, None),
            P("ctx", "resp"),
            P(),
            P(),
            P(),
            P(),
            P(),
            P("ctx", "resp", None),
            P("ctx", "resp", None),
            P("ctx", "resp", None, None),
            P("ctx", "resp", None, None),
        ),
        out_specs=(P("ctx", "resp", None), P("ctx", "resp", None, None), P(), P(), P(), P(), P()),
        check_vma=False,
    )
```

```python
import functools

import jax
import jax.numpy as jnp
import numpy as np
from jax import lax
from jax.experimental import pallas as pl
from jax.experimental.pallas import tpu as pltpu
from jax.sharding import Mesh
from jax.sharding import PartitionSpec as P

HEAD_DIM = 128
HALF = 64
RANK = 16
ROPE_BASE = 1000000.0
LOG2E = 1.4426950408889634
F32 = jnp.float32
BF16 = jnp.bfloat16
CTX = ("x", "z_hi")
RESP = ("z_lo", "y", "core")
CHIPS = ("x", "z_hi", "z_lo", "y")
SIZES = (4, 2, 2, 4, 2)
PAIR = [(0, 1), (1, 0)]

NN = (((1,), (0,)), ((), ()))
NT = (((1,), (1,)), ((), ()))
TN = (((0,), (0,)), ((), ()))


def mm(a, b, dims=NN):
    return lax.dot_general(a, b, dims, preferred_element_type=F32)


def rope_tables(count):
    rates = ROPE_BASE ** (-(np.arange(HALF, dtype=np.float64) * (2.0 / HEAD_DIM)))
    angle = np.arange(count, dtype=np.float64)[:, None] * rates[None, :]
    return np.cos(angle), np.sin(angle)


def rope(x, cos, sin):
    return x * cos + pltpu.roll(x, HALF, 1) * sin


def unrope(x, cos, sin):
    return x * cos - pltpu.roll(x, HALF, 1) * sin


def params(flops=0, nbytes=0, mib=36):
    return dict(
        compiler_params=pltpu.CompilerParams(vmem_limit_bytes=mib * 1024 * 1024),
        cost_estimate=pl.CostEstimate(flops=flops, bytes_accessed=nbytes, transcendentals=0),
    )


def kv_rows(hidden, base, down, kv_up, cos, sin):
    kv_width = kv_up.shape[2]
    low = mm(hidden, down, NT).astype(BF16)
    zero = jnp.zeros((RANK, kv_width), BF16)
    k_lift = jnp.concatenate([zero, kv_up[0], zero], axis=0)
    v_lift = jnp.concatenate([zero, zero, kv_up[1]], axis=0)
    key = base[:, :kv_width].astype(F32) + 2.0 * mm(low, k_lift)
    value = base[:, kv_width:].astype(F32) + 2.0 * mm(low, v_lift)
    heads = [
        rope(key[:, h : h + HEAD_DIM], cos, sin).astype(BF16)
        for h in range(0, kv_width, HEAD_DIM)
    ]
    return low, jnp.concatenate(heads, axis=1), value.astype(BF16)


def pad_low(low):
    return jnp.concatenate([low, jnp.zeros((low.shape[0], HEAD_DIM - 3 * RANK), BF16)], axis=1)


def front_kernel(spot, hidden, base, down, kv_up, cos, sin, out):
    low, key, value = kv_rows(hidden[0], base[0], down[...], kv_up[...], cos[...], sin[...])
    half = key.shape[1] // 2
    out[...] = jnp.concatenate(
        [key[:, :half], value[:, :half], pad_low(low), key[:, half:], value[:, half:]], axis=1
    )


def reply_kernel(
    lengths, p_low, p_out, r_hidden, r_base, r_out, down, kv_up, out_up, r_cos, r_sin,
    r_kv, lows, splits, low_t, lowered_t,
):
    pr = p_low.shape[0]
    rl = r_hidden.shape[2]
    r_low, r_key, r_value = kv_rows(
        r_hidden[0, 0], r_base[0, 0], down[...], kv_up[...], r_cos[...], r_sin[...]
    )
    r_low = pad_low(r_low)
    r_kv[...] = jnp.concatenate([r_key, r_value, r_low], axis=1)
    live = lax.broadcasted_iota(jnp.int32, (rl, RANK), 0) < lengths[0, 0]
    p_lowered = mm(p_out[0], out_up[...], NT)
    r_lowered = jnp.where(live, mm(r_out[0, 0], out_up[...], NT), 0.0)
    for low, lowered, at, n in ((p_low[...], p_lowered, 0, pr), (r_low, r_lowered, pr, rl)):
        lows[at : at + n, :] = low
        low_t[:, pl.ds(at, n)] = jnp.transpose(low.astype(F32))[: 3 * RANK].astype(BF16)
        high = lowered.astype(BF16)
        lost = (lowered - high.astype(F32)).astype(BF16)
        zero = jnp.zeros((n, HEAD_DIM - 2 * RANK), BF16)
        both = jnp.concatenate([high, lost, zero], axis=1)
        splits[at : at + n, :] = both
        lowered_t[:, pl.ds(at, n)] = jnp.transpose(both.astype(F32))[: 2 * RANK].astype(BF16)


def query_kernel(
    spot, lengths, lows, splits, p_base, p_gbase, r_base, r_gbase, q_up, out_down,
    p_cos, p_sin, r_cos, r_sin, query, push,
):
    pr = p_base.shape[1]
    rl = r_base.shape[2]
    wide = q_up.shape[1]
    live = lax.broadcasted_iota(jnp.int32, (rl, wide), 0) < lengths[0, 0]
    q_lift = jnp.concatenate([q_up[...], jnp.zeros((HEAD_DIM - RANK, wide), BF16)], axis=0)
    o_lift = jnp.concatenate(
        [out_down[...], out_down[...], jnp.zeros((HEAD_DIM - 2 * RANK, wide), BF16)], axis=0
    )
    for base, gbase, cos, sin, at, n in (
        (p_base[0], p_gbase[0], p_cos, p_sin, 0, pr),
        (r_base[0, 0], r_gbase[0, 0], r_cos, r_sin, pr, rl),
    ):
        q = base.astype(F32) + 2.0 * mm(lows[at : at + n, :], q_lift)
        for h in range(0, wide, HEAD_DIM):
            query[at : at + n, h : h + HEAD_DIM] = rope(
                q[:, h : h + HEAD_DIM], cos[...], sin[...]
            ).astype(BF16)
        up = gbase.astype(F32) + 2.0 * mm(splits[at : at + n, :], o_lift)
        if at:
            up = jnp.where(live, up, 0.0)
        push[at : at + n, :] = up.astype(BF16)


def attend_kernel(
    first, spot, lengths, query, push, key_a, key_b, value_a, value_b, low_a, low_b,
    r_key, r_value, r_low, low_t, lowered_t,
    q_up, kv_up, out_down, p_cos, p_sin, r_cos, r_sin, cos_t, sin_t, *others,
):
    if not first:
        fold_q_in, lifted_in, fold_kv_in, _, _ = others[:5]
        others = others[5:]
    (
        p_context, r_context, tiles, fold_q, lifted, fold_kv, fold_send, fold_reply,
        dk_t, dv_t, raw_q, mixed, keys, values, lows, bias,
    ) = others
    pr = p_context.shape[1]
    rl = r_context.shape[2]
    prompt = bias.shape[1]
    scale = HEAD_DIM ** (-0.5)
    step = scale * LOG2E
    heads = key_a.shape[1] // HEAD_DIM
    wide = query.shape[1] // heads
    share = wide // HEAD_DIM
    block = 512

    me = spot[0]
    places = []
    for other in (0, 1):
        for j in range(8):
            away, far = j // 2, j % 2
            z = jnp.bitwise_xor(me >> 3, far)
            y = jnp.bitwise_and((me >> 1) - away + 4, 3)
            c = jnp.bitwise_xor(jnp.bitwise_and(me, 1), other)
            places.append((other, j, pl.ds(pl.multiple_of((z * 8 + y * 2 + c) * pr, pr), pr)))

    row = lax.broadcasted_iota(jnp.int32, (pr, prompt), 0) + spot[0] * pr
    col = lax.broadcasted_iota(jnp.int32, (pr, prompt), 1)
    bias[...] = jnp.where(col <= row, 0.0, -jnp.inf)
    for other, j, rows in places:
        part = slice(j * pr, (j + 1) * pr)
        lows[rows, :] = (low_a, low_b)[other][part, :]
        for g in range(heads):
            cols = slice(g * HEAD_DIM, (g + 1) * HEAD_DIM)
            keys[g, rows, :] = (key_a, key_b)[other][part, cols]
            values[g, rows, :HEAD_DIM] = (value_a, value_b)[other][part, cols]
    lows[prompt:, :] = r_low[...]
    for g in range(heads):
        cols = slice(g * HEAD_DIM, (g + 1) * HEAD_DIM)
        keys[g, prompt:, :] = r_key[:, cols]
        values[g, prompt:, :HEAD_DIM] = r_value[:, cols]
        values[g, :, HEAD_DIM:] = jnp.ones((prompt + rl, HEAD_DIM), BF16)
    dk_t[...] = jnp.zeros_like(dk_t)
    dv_t[...] = jnp.zeros_like(dv_t)

    def stages(g, n, at, of, mask, keep, cos, sin, count):
        def stack(ref):
            return jnp.concatenate(
                [ref[at : at + n, h * HEAD_DIM : (h + 1) * HEAD_DIM] for h in of], axis=0
            )

        box = {}

        def scores():
            box["q"], box["p"] = stack(query), stack(push)
            box["score"] = mask(mm(box["q"], keys[g, :count, :], NT))

        def softmax():
            score = box.pop("score")
            top = jnp.max(score, axis=1, keepdims=True) * step
            box["weight"] = jnp.exp2(score * step - top).astype(BF16)

        def mix():
            box["summed"] = mm(box["weight"], values[g, :count, :])
            box["dprob"] = mm(box["p"], values[g, :count, :HEAD_DIM], NT)

        def backward():
            summed = box.pop("summed")
            share_of = 1.0 / summed[:, HEAD_DIM:]
            p = box.pop("p").astype(F32)
            context = keep((summed[:, :HEAD_DIM] * share_of).astype(BF16))
            delta = jnp.sum(context.astype(F32) * p, axis=1, keepdims=True)
            box["dscore"] = (box["weight"].astype(F32) * (box.pop("dprob") - delta)).astype(BF16)
            box["inverse"] = share_of * scale
            box["ps"] = (p * share_of).astype(BF16)
            box["qs"] = (box.pop("q").astype(F32) * box["inverse"]).astype(BF16)
            for i, h in enumerate(of):
                part = slice(i * n, (i + 1) * n)
                mixed[at : at + n, h * HEAD_DIM : (h + 1) * HEAD_DIM] = context[part]

        def products():
            dscore = box.pop("dscore")
            dv_t[g, :, :count] += mm(box.pop("ps"), box.pop("weight"), TN)
            dq = mm(dscore, keys[g, :count, :]) * box.pop("inverse")
            dk_t[g, :, :count] += mm(box.pop("qs"), dscore, TN)
            for i, h in enumerate(of):
                part = slice(i * n, (i + 1) * n)
                raw_q[at : at + n, h * HEAD_DIM : (h + 1) * HEAD_DIM] = unrope(
                    dq[part], cos[...], sin[...]
                ).astype(BF16)

        return scores, softmax, mix, backward, products

    p_heads = block // pr
    r_heads = block // rl

    def p_mask(score):
        seen = bias[...]
        return jnp.concatenate(
            [score[i * pr : (i + 1) * pr] + seen for i in range(p_heads)], axis=0
        )

    r_row = lax.broadcasted_iota(jnp.int32, (rl, rl), 0)
    r_col = lax.broadcasted_iota(jnp.int32, (rl, rl), 1)
    r_seen = jnp.concatenate([r_col <= r_row] * r_heads, axis=0)
    live = jnp.concatenate([r_row < lengths[0, 0]] * r_heads, axis=0)

    def r_mask(score):
        own = jnp.where(r_seen, score[:, prompt:], -jnp.inf)
        return jnp.concatenate([score[:, :prompt], own], axis=1)

    def finish(g):
        cols = slice(g * wide, (g + 1) * wide)
        context = mixed[:, cols]
        raw = raw_q[:, cols]
        p_context[0, :, cols] = mixed[:pr, cols]
        r_context[0, 0, :, cols] = mixed[pr:, cols]
        gq = (2.0 * mm(low_t[:RANK, :], raw)).astype(BF16)
        both = mm(lowered_t[...], context)
        god = (2.0 * (both[:RANK] + both[RANK:])).astype(BF16)
        first_tile = g * (2 * share + 2)
        for t in range(share):
            at = slice(t * HEAD_DIM, (t + 1) * HEAD_DIM)
            tiles[first_tile + t] = gq[:, at]
            tiles[first_tile + share + t] = god[:, at]
        upper, lower = dk_t[g, :HALF, :], dk_t[g, HALF:, :]
        cos, sin = cos_t[...], sin_t[...]
        raw_k = jnp.concatenate(
            [(upper * cos + lower * sin).astype(BF16), (lower * cos - upper * sin).astype(BF16)],
            axis=0,
        )
        raw_v = dv_t[g].astype(BF16)
        head = slice(g * HEAD_DIM, (g + 1) * HEAD_DIM)
        gk = jnp.transpose(mm(raw_k, lows[...]))
        gv = jnp.transpose(mm(raw_v, lows[...]))
        tiles[first_tile + 2 * share] = (2.0 * gk[RANK : 2 * RANK]).astype(BF16)
        tiles[first_tile + 2 * share + 1] = (2.0 * gv[2 * RANK : 3 * RANK]).astype(BF16)
        return (
            mm(q_up[:, cols], raw, NT),
            mm(out_down[:, cols], context, NT),
            mm(kv_up[0, :, head], raw_k),
            mm(kv_up[1, :, head], raw_v),
        )

    blocks = []
    for g in range(heads):
        for b in range(share // p_heads):
            of = [g * share + b * p_heads + i for i in range(p_heads)]
            blocks.append(stages(g, pr, 0, of, p_mask, lambda c: c, p_cos, p_sin, prompt))
        for b in range(share // r_heads):
            of = [g * share + b * r_heads + i for i in range(r_heads)]
            blocks.append(
                stages(
                    g, rl, pr, of, r_mask, lambda c: jnp.where(live, c, jnp.zeros_like(c)),
                    r_cos, r_sin, prompt + rl,
                )
            )
    each = len(blocks) // heads
    if first:
        folds = None
    else:
        folds = [fold_q_in[...], lifted_in[...], fold_kv_in[:RANK, :], fold_kv_in[RANK:, :]]
    for at in range(len(blocks) + 1):
        if at < len(blocks):
            blocks[at][0]()
        if at:
            blocks[at - 1][3]()
            blocks[at - 1][4]()
        if at < len(blocks):
            blocks[at][1]()
            blocks[at][2]()
        if at and at % each == 0:
            new = finish(at // each - 1)
            folds = new if folds is None else [x + y for x, y in zip(folds, new)]
    fold_q[...] = folds[0]
    lifted[...] = folds[1]
    fk, fv = folds[2], folds[3]
    fold_kv[:RANK, :] = fk
    fold_kv[RANK:, :] = fv
    for r in range(prompt // pr):
        cols = slice(r * pr, (r + 1) * pr)
        fold_send[r] = jnp.concatenate([fk[:, cols], fv[:, cols]], axis=1).astype(BF16)
    fold_reply[...] = jnp.concatenate([fk[:, prompt:], fv[:, prompt:]], axis=0).astype(BF16)


def grads_kernel(
    spot, fold_q, lifted, fold_reply, fold_recv, p_hidden, r_hidden, p_out, r_out, tiles_a, tiles_b,
    keep, give, held,
):
    pr = p_hidden.shape[1]
    fq = fold_q[...].astype(BF16)
    up = lifted[...].astype(BF16)
    own = jnp.sum(fold_recv[...].astype(F32), axis=0).astype(BF16)
    fp = jnp.concatenate([fq[:, :pr], own[:, :pr], own[:, pr:]], axis=0)
    fr = jnp.concatenate([fq[:, pr:], fold_reply[...]], axis=0)
    wide = p_hidden.shape[2] // HEAD_DIM
    down = (2.0 * (mm(fp, p_hidden[0]) + mm(fr, r_hidden[0, 0]))).astype(BF16)
    grad_up = (2.0 * (mm(up[:, :pr], p_out[0]) + mm(up[:, pr:], r_out[0, 0]))).astype(BF16)
    for t in range(wide):
        cols = slice(t * HEAD_DIM, (t + 1) * HEAD_DIM)
        for j in range(3):
            held[j * wide + t] = down[j * RANK : (j + 1) * RANK, cols]
        held[3 * wide + t] = grad_up[:, cols]
    at = 4 * wide
    small = tiles_a.shape[0]
    held[at : at + small] = tiles_a[...]
    held[at + small : at + 2 * small] = tiles_b[...]
    left = held.shape[0] - at - 2 * small
    held[at + 2 * small :] = jnp.zeros((left, RANK, HEAD_DIM), BF16)
    half = held.shape[0] // 2
    core = jnp.bitwise_and(spot[0], 1)

    @pl.when(core == 0)
    def _():
        keep[...] = held[:half]
        give[...] = held[half:]

    @pl.when(core == 1)
    def _():
        keep[...] = held[half:]
        give[...] = held[:half]


def unpack_kernel(spot, mine, theirs, down, gq, gkv, god, up, held):
    half = mine.shape[0]
    core = jnp.bitwise_and(spot[0], 1)

    @pl.when(core == 0)
    def _():
        held[:half] = mine[...]
        held[half:] = theirs[...]

    @pl.when(core == 1)
    def _():
        held[half:] = mine[...]
        held[:half] = theirs[...]

    def cols(t):
        return slice(t * HEAD_DIM, (t + 1) * HEAD_DIM)

    wide = down.shape[1] // HEAD_DIM
    for t in range(wide):
        for j in range(3):
            down[j * RANK : (j + 1) * RANK, cols(t)] = held[j * wide + t].astype(F32)
        up[:, cols(t)] = held[3 * wide + t].astype(F32)
    at = 4 * wide
    heads = gkv.shape[1] // HEAD_DIM
    share = gq.shape[1] // HEAD_DIM // heads
    for g in range(heads):
        for t in range(share):
            gq[:, cols(g * share + t)] = held[at + t].astype(F32)
            god[:, cols(g * share + t)] = held[at + share + t].astype(F32)
        gkv[:RANK, cols(g)] = held[at + 2 * share].astype(F32)
        gkv[RANK:, cols(g)] = held[at + 2 * share + 1].astype(F32)
        at += 2 * share + 2


def whole(shape):
    return pl.BlockSpec(shape, lambda *_: (0,) * len(shape))


def shifted(x, axis, by):
    n = lax.axis_size(axis)
    return lax.ppermute(x, axis, [(i, (i + by) % n) for i in range(n)])


def chips_of(pair):
    return [pair] + [shifted(pair, "y", k) for k in (1, 2, 3)]


def per_device(
    prompt_hidden,
    prompt_base,
    reply_hidden,
    reply_base,
    reply_lengths,
    adapter_down,
    query_up_weight,
    key_value_up_weight,
    output_down,
    output_up,
    prompt_grad_out,
    prompt_grad_base,
    reply_grad_out,
    reply_grad_base,
):
    group = lax.axis_size(RESP)
    pr = prompt_hidden.shape[1]
    rl = reply_hidden.shape[2]
    d = prompt_hidden.shape[2]
    prompt = pr * group
    q_width = query_up_weight.shape[1]
    kv_width = key_value_up_weight.shape[2]
    heads = kv_width // HEAD_DIM
    each = heads // 2
    qb = q_width // heads
    share = qb // HEAD_DIM
    rows = pr + rl
    wide = 2 * kv_width + HEAD_DIM
    low_at = 2 * kv_width // HEAD_DIM

    spot = lax.axis_index(RESP).astype(jnp.int32)[None]
    down = jnp.transpose(adapter_down, (0, 2, 1)).reshape(3 * RANK, d)
    out_down = jnp.transpose(output_down)
    cos, sin = rope_tables(prompt + rl)
    cos_rows = jnp.asarray(np.concatenate([cos, cos], axis=1), F32)
    sin_rows = jnp.asarray(np.concatenate([-sin, sin], axis=1), F32)
    cos_t = jnp.asarray(cos.T, F32)
    sin_t = jnp.asarray(sin.T, F32)
    p_table = pl.BlockSpec((pr, HEAD_DIM), lambda i, s: (s[0], 0))
    r_table = pl.BlockSpec((rl, HEAD_DIM), lambda i, *_: (prompt // rl, 0))

    own_kv = pl.pallas_call(
        front_kernel,
        grid_spec=pltpu.PrefetchScalarGridSpec(
            num_scalar_prefetch=1,
            grid=(1,),
            in_specs=[
                whole((1, pr, d)),
                pl.BlockSpec((1, pr, 2 * kv_width), lambda i, s: (0, 0, q_width // (2 * kv_width))),
                whole((3 * RANK, d)),
                whole((2, RANK, kv_width)),
                p_table,
                p_table,
            ],
            out_specs=whole((pr, wide)),
        ),
        out_shape=jax.ShapeDtypeStruct((pr, wide), BF16),
        name="front",
        **params(2 * pr * d * 48, 2_000_000, 56),
    )(spot, prompt_hidden, prompt_base, down, key_value_up_weight, cos_rows, sin_rows)

    far_kv = lax.ppermute(own_kv, "z_lo", PAIR)

    reply_kv, lows, splits, low_t, lowered_t = pl.pallas_call(
        reply_kernel,
        grid=(1,),
        in_specs=[
            pl.BlockSpec(memory_space=pltpu.SMEM),
            pl.BlockSpec((pr, HEAD_DIM), lambda i: (0, kv_width // HEAD_DIM)),
            whole((1, pr, d)),
            whole((1, 1, rl, d)),
            pl.BlockSpec(
                (1, 1, rl, 2 * kv_width), lambda i: (0, 0, 0, q_width // (2 * kv_width))
            ),
            whole((1, 1, rl, d)),
            whole((3 * RANK, d)),
            whole((2, RANK, kv_width)),
            whole((RANK, d)),
            r_table,
            r_table,
        ],
        out_specs=[
            whole((rl, wide)),
            whole((rows, HEAD_DIM)),
            whole((rows, HEAD_DIM)),
            whole((3 * RANK, rows)),
            whole((2 * RANK, rows)),
        ],
        out_shape=[
            jax.ShapeDtypeStruct((rl, wide), BF16),
            jax.ShapeDtypeStruct((rows, HEAD_DIM), BF16),
            jax.ShapeDtypeStruct((rows, HEAD_DIM), BF16),
            jax.ShapeDtypeStruct((3 * RANK, rows), BF16),
            jax.ShapeDtypeStruct((2 * RANK, rows), BF16),
        ],
        name="reply",
        **params(4 * rows * d * 48, 6_000_000, 56),
    )(
        reply_lengths, own_kv, prompt_grad_out, reply_hidden, reply_base, reply_grad_out, down,
        key_value_up_weight, output_up, cos_rows, sin_rows,
    )

    own_kv, far_kv, lows, splits = lax.optimization_barrier((own_kv, far_kv, lows, splits))
    cut = kv_width + HEAD_DIM
    first_pair = jnp.concatenate([own_kv[:, :cut], far_kv[:, :cut]], axis=0)
    second_pair = jnp.concatenate([own_kv[:, cut:], far_kv[:, cut:]], axis=0)
    first_parts = chips_of(first_pair)

    def head_cols(n, width, shift=0):
        return pl.BlockSpec((n, width), lambda i, s: (0, i + shift))

    def cols3(shift=0):
        return pl.BlockSpec((1, pr, qb), lambda i, s: (0, 0, i + shift))

    def cols4(shift=0):
        return pl.BlockSpec((1, 1, rl, qb), lambda i, s: (0, 0, 0, i + shift))

    query, push = pl.pallas_call(
        query_kernel,
        grid_spec=pltpu.PrefetchScalarGridSpec(
            num_scalar_prefetch=1,
            grid=(heads,),
            in_specs=[
                pl.BlockSpec(memory_space=pltpu.SMEM),
                whole((rows, HEAD_DIM)),
                whole((rows, HEAD_DIM)),
                cols3(),
                cols3(),
                cols4(),
                cols4(),
                head_cols(RANK, qb),
                head_cols(RANK, qb),
                p_table,
                p_table,
                r_table,
                r_table,
            ],
            out_specs=[head_cols(rows, qb), head_cols(rows, qb)],
        ),
        out_shape=[
            jax.ShapeDtypeStruct((rows, q_width), BF16),
            jax.ShapeDtypeStruct((rows, q_width), BF16),
        ],
        name="query",
        **params(4 * rows * q_width * 128, 8_000_000, 48),
    )(
        spot, reply_lengths, lows, splits, prompt_base, prompt_grad_base, reply_base,
        reply_grad_base, query_up_weight, out_down, cos_rows, sin_rows, cos_rows, sin_rows,
    )

    first_parts, second_pair, query, push = lax.optimization_barrier(
        (first_parts, second_pair, query, push)
    )
    first_own = jnp.concatenate(first_parts, axis=0)
    first_other = lax.ppermute(first_own, "core", PAIR)
    second_parts = chips_of(second_pair)
    count = prompt // 2
    low_block = pl.BlockSpec((count, HEAD_DIM), lambda i, s: (0, kv_width // HEAD_DIM))

    def attend(own, other, at, before):
        first = before is None
        kb = each * HEAD_DIM
        in_specs = [
            pl.BlockSpec(memory_space=pltpu.SMEM),
            head_cols(rows, each * qb, at),
            head_cols(rows, each * qb, at),
            head_cols(count, kb),
            head_cols(count, kb),
            head_cols(count, kb, 1),
            head_cols(count, kb, 1),
            low_block,
            low_block,
            head_cols(rl, kb, at),
            head_cols(rl, kb, heads // each + at),
            pl.BlockSpec((rl, HEAD_DIM), lambda i, s: (0, low_at)),
            whole((3 * RANK, rows)),
            whole((2 * RANK, rows)),
            head_cols(RANK, each * qb, at),
            pl.BlockSpec((2, RANK, kb), lambda i, s: (0, 0, i + at)),
            head_cols(RANK, each * qb, at),
            p_table,
            p_table,
            r_table,
            r_table,
            whole((HALF, prompt + rl)),
            whole((HALF, prompt + rl)),
        ]
        operands = [
            spot, reply_lengths, query, push, own, other, own, other, first_own, first_other,
            reply_kv, reply_kv, reply_kv, low_t, lowered_t, query_up_weight, key_value_up_weight,
            out_down, cos_rows, sin_rows, cos_rows, sin_rows, cos_t, sin_t,
        ]
        aliases = {}
        if not first:
            aliases = {len(operands) + 3: 0, len(operands) + 4: 1}
            in_specs += [
                whole((RANK, rows)),
                whole((RANK, rows)),
                whole((2 * RANK, prompt + rl)),
                pl.BlockSpec(memory_space=pl.ANY),
                pl.BlockSpec(memory_space=pl.ANY),
            ]
            operands += list(before)
        per_head = 2 * share + 2
        return pl.pallas_call(
            functools.partial(attend_kernel, first),
            grid_spec=pltpu.PrefetchScalarGridSpec(
                num_scalar_prefetch=1,
                grid=(1,),
                in_specs=in_specs,
                out_specs=[
                    pl.BlockSpec((1, pr, each * qb), lambda i, s: (0, 0, i + at)),
                    pl.BlockSpec((1, 1, rl, each * qb), lambda i, s: (0, 0, 0, i + at)),
                    whole((each * per_head, RANK, HEAD_DIM)),
                    whole((RANK, rows)),
                    whole((RANK, rows)),
                    whole((2 * RANK, prompt + rl)),
                    whole((group, RANK, 2 * pr)),
                    whole((2 * RANK, rl)),
                ],
                scratch_shapes=[
                    pltpu.VMEM((each, HEAD_DIM, prompt + rl), F32),
                    pltpu.VMEM((each, HEAD_DIM, prompt + rl), F32),
                    pltpu.VMEM((rows, each * qb), BF16),
                    pltpu.VMEM((rows, each * qb), BF16),
                    pltpu.VMEM((each, prompt + rl, HEAD_DIM), BF16),
                    pltpu.VMEM((each, prompt + rl, 2 * HEAD_DIM), BF16),
                    pltpu.VMEM((prompt + rl, HEAD_DIM), BF16),
                    pltpu.VMEM((pr, prompt), F32),
                ],
            ),
            out_shape=[
                jax.ShapeDtypeStruct((1, pr, q_width), BF16),
                jax.ShapeDtypeStruct((1, 1, rl, q_width), BF16),
                jax.ShapeDtypeStruct((each * per_head, RANK, HEAD_DIM), BF16),
                jax.ShapeDtypeStruct((RANK, rows), F32),
                jax.ShapeDtypeStruct((RANK, rows), F32),
                jax.ShapeDtypeStruct((2 * RANK, prompt + rl), F32),
                jax.ShapeDtypeStruct((group, RANK, 2 * pr), BF16),
                jax.ShapeDtypeStruct((2 * RANK, rl), BF16),
            ],
            input_output_aliases=aliases,
            name="attend",
            **params(12 * rows * prompt * q_width // 2, 8_000_000),
        )(*operands)

    p_half, r_half, tiles_a, fold_q, lifted, fold_kv, _, _ = attend(
        first_own, first_other, 0, None
    )
    second_parts, fold_q, lifted, fold_kv = lax.optimization_barrier(
        (second_parts, fold_q, lifted, fold_kv)
    )
    second_own = jnp.concatenate(second_parts, axis=0)
    second_other = lax.ppermute(second_own, "core", PAIR)
    p_context, r_context, tiles_b, fold_q, lifted, _, fold_send, fold_reply = attend(
        second_own, second_other, 1, (fold_q, lifted, fold_kv, p_half, r_half)
    )

    fold_recv = lax.all_to_all(fold_send, RESP, 0, 0, tiled=True)

    slots = 2 * lax.axis_size(CHIPS) * 2
    half = slots // 2
    keep, give = pl.pallas_call(
        grads_kernel,
        grid_spec=pltpu.PrefetchScalarGridSpec(
            num_scalar_prefetch=1,
            grid=(1,),
            in_specs=[
                whole((RANK, rows)),
                whole((RANK, rows)),
                whole((2 * RANK, rl)),
                whole((group, RANK, 2 * pr)),
                whole((1, pr, d)),
                whole((1, 1, rl, d)),
                whole((1, pr, d)),
                whole((1, 1, rl, d)),
                whole(tiles_a.shape),
                whole(tiles_b.shape),
            ],
            out_specs=[whole((half, RANK, HEAD_DIM)), whole((half, RANK, HEAD_DIM))],
            scratch_shapes=[pltpu.VMEM((slots, RANK, HEAD_DIM), BF16)],
        ),
        out_shape=[jax.ShapeDtypeStruct((half, RANK, HEAD_DIM), BF16)] * 2,
        name="grads",
        **params(2 * rows * d * 64, 5_000_000),
    )(
        spot, fold_q, lifted, fold_reply, fold_recv, prompt_hidden, reply_hidden, prompt_grad_out,
        reply_grad_out, tiles_a, tiles_b,
    )

    chips = lax.axis_size(CHIPS)
    got = lax.ppermute(give, "core", PAIR)
    paired = (keep.astype(F32) + got.astype(F32)).astype(BF16)
    spread = lax.all_to_all(
        paired.reshape(chips, -1, HEAD_DIM), CHIPS, 0, 0, tiled=True
    )
    total = jnp.sum(spread.astype(F32), axis=0).astype(BF16)
    mine = lax.all_to_all(
        jnp.broadcast_to(total[None], spread.shape), CHIPS, 0, 0, tiled=True
    ).reshape(half, RANK, HEAD_DIM)
    theirs = lax.ppermute(mine, "core", PAIR)

    shapes = [(3 * RANK, d), (RANK, q_width), (2 * RANK, kv_width), (RANK, q_width), (RANK, d)]
    sum_down, sum_q, sum_kv, sum_od, sum_up = pl.pallas_call(
        unpack_kernel,
        grid_spec=pltpu.PrefetchScalarGridSpec(
            num_scalar_prefetch=1,
            grid=(1,),
            in_specs=[whole((half, RANK, HEAD_DIM))] * 2,
            out_specs=[whole(x) for x in shapes],
            scratch_shapes=[pltpu.VMEM((slots, RANK, HEAD_DIM), BF16)],
        ),
        out_shape=[jax.ShapeDtypeStruct(x, F32) for x in shapes],
        name="unpack",
        **params(0, 3_000_000),
    )(spot, mine, theirs)
    return (
        p_context,
        r_context,
        jnp.transpose(sum_down.reshape(3, RANK, d), (0, 2, 1)),
        sum_q,
        sum_kv.reshape(2, RANK, kv_width),
        jnp.transpose(sum_od),
        sum_up,
    )


def solution(mesh):
    fine = Mesh(mesh.devices.reshape(SIZES), CTX + RESP)
    return jax.shard_map(
        per_device,
        mesh=fine,
        in_specs=(
            P(CTX, RESP, None),
            P(CTX, RESP, None),
            P(CTX, RESP, None, None),
            P(CTX, RESP, None, None),
            P(CTX, RESP),
            P(),
            P(),
            P(),
            P(),
            P(),
            P(CTX, RESP, None),
            P(CTX, RESP, None),
            P(CTX, RESP, None, None),
            P(CTX, RESP, None, None),
        ),
        out_specs=(P(CTX, RESP, None), P(CTX, RESP, None, None), P(), P(), P(), P(), P()),
        check_vma=False,
    )
```

```python
import functools

import jax
import jax.numpy as jnp
import numpy as np
from jax import lax
from jax.experimental import pallas as pl
from jax.experimental.pallas import tpu as pltpu
from jax.sharding import Mesh
from jax.sharding import PartitionSpec as P

HEAD_DIM = 128
HALF = 64
RANK = 16
ROPE_BASE = 1000000.0
LOG2E = 1.4426950408889634
F32 = jnp.float32
BF16 = jnp.bfloat16
CTX = ("x", "z_hi")
RESP = ("z_lo", "y", "core")
CHIPS = ("x", "z_hi", "z_lo", "y")
SIZES = (4, 2, 2, 4, 2)
PAIR = [(0, 1), (1, 0)]

NN = (((1,), (0,)), ((), ()))
NT = (((1,), (1,)), ((), ()))
TN = (((0,), (0,)), ((), ()))


def mm(a, b, dims=NN):
    return lax.dot_general(a, b, dims, preferred_element_type=F32)


def rope_tables(count):
    rates = ROPE_BASE ** (-(np.arange(HALF, dtype=np.float64) * (2.0 / HEAD_DIM)))
    angle = np.arange(count, dtype=np.float64)[:, None] * rates[None, :]
    return np.cos(angle), np.sin(angle)


def rope(x, cos, sin):
    return x * cos + pltpu.roll(x, HALF, 1) * sin


def unrope(x, cos, sin):
    return x * cos - pltpu.roll(x, HALF, 1) * sin


def params(flops=0, nbytes=0, mib=36):
    return dict(
        compiler_params=pltpu.CompilerParams(vmem_limit_bytes=mib * 1024 * 1024),
        cost_estimate=pl.CostEstimate(flops=flops, bytes_accessed=nbytes, transcendentals=0),
    )


def kv_rows(hidden, base, down, kv_up, cos, sin):
    kv_width = kv_up.shape[2]
    low = mm(hidden, down, NT).astype(BF16)
    zero = jnp.zeros((RANK, kv_width), BF16)
    k_lift = jnp.concatenate([zero, kv_up[0], zero], axis=0)
    v_lift = jnp.concatenate([zero, zero, kv_up[1]], axis=0)
    key = base[:, :kv_width].astype(F32) + 2.0 * mm(low, k_lift)
    value = base[:, kv_width:].astype(F32) + 2.0 * mm(low, v_lift)
    heads = [
        rope(key[:, h : h + HEAD_DIM], cos, sin).astype(BF16)
        for h in range(0, kv_width, HEAD_DIM)
    ]
    return low, jnp.concatenate(heads, axis=1), value.astype(BF16)


def pad_low(low):
    return jnp.concatenate([low, jnp.zeros((low.shape[0], HEAD_DIM - 3 * RANK), BF16)], axis=1)


def front_kernel(spot, hidden, base, down, kv_up, cos, sin, out):
    low, key, value = kv_rows(hidden[0], base[0], down[...], kv_up[...], cos[...], sin[...])
    half = key.shape[1] // 2
    out[...] = jnp.concatenate(
        [key[:, :half], value[:, :half], pad_low(low), key[:, half:], value[:, half:]], axis=1
    )


def reply_kernel(
    lengths, p_low, p_out, r_hidden, r_base, r_out, down, kv_up, out_up, r_cos, r_sin,
    r_kv, lows, splits, low_t, lowered_t,
):
    pr = p_low.shape[0]
    rl = r_hidden.shape[2]
    r_low, r_key, r_value = kv_rows(
        r_hidden[0, 0], r_base[0, 0], down[...], kv_up[...], r_cos[...], r_sin[...]
    )
    r_low = pad_low(r_low)
    r_kv[...] = jnp.concatenate([r_key, r_value, r_low], axis=1)
    live = lax.broadcasted_iota(jnp.int32, (rl, RANK), 0) < lengths[0, 0]
    p_lowered = mm(p_out[0], out_up[...], NT)
    r_lowered = jnp.where(live, mm(r_out[0, 0], out_up[...], NT), 0.0)
    for low, lowered, at, n in ((p_low[...], p_lowered, 0, pr), (r_low, r_lowered, pr, rl)):
        lows[at : at + n, :] = low
        low_t[:, pl.ds(at, n)] = jnp.transpose(low.astype(F32))[: 3 * RANK].astype(BF16)
        high = lowered.astype(BF16)
        lost = (lowered - high.astype(F32)).astype(BF16)
        zero = jnp.zeros((n, HEAD_DIM - 2 * RANK), BF16)
        both = jnp.concatenate([high, lost, zero], axis=1)
        splits[at : at + n, :] = both
        lowered_t[:, pl.ds(at, n)] = jnp.transpose(both.astype(F32))[: 2 * RANK].astype(BF16)


def query_kernel(
    spot, lengths, lows, splits, p_base, p_gbase, r_base, r_gbase, q_up, out_down,
    p_cos, p_sin, r_cos, r_sin, query_a, push_a, query_b, push_b, mark,
):
    mark[...] = splits[: mark.shape[0], :]
    pr = p_base.shape[1]
    rl = r_base.shape[2]
    wide = q_up.shape[1]
    live = lax.broadcasted_iota(jnp.int32, (rl, wide), 0) < lengths[0, 0]
    q_lift = jnp.concatenate([q_up[...], jnp.zeros((HEAD_DIM - RANK, wide), BF16)], axis=0)
    o_lift = jnp.concatenate(
        [out_down[...], out_down[...], jnp.zeros((HEAD_DIM - 2 * RANK, wide), BF16)], axis=0
    )
    def fill(query, push):
        for base, gbase, cos, sin, at, n in (
            (p_base[0], p_gbase[0], p_cos, p_sin, 0, pr),
            (r_base[0, 0], r_gbase[0, 0], r_cos, r_sin, pr, rl),
        ):
            q = base.astype(F32) + 2.0 * mm(lows[at : at + n, :], q_lift)
            for h in range(0, wide, HEAD_DIM):
                query[at : at + n, h : h + HEAD_DIM] = rope(
                    q[:, h : h + HEAD_DIM], cos[...], sin[...]
                ).astype(BF16)
            up = gbase.astype(F32) + 2.0 * mm(splits[at : at + n, :], o_lift)
            if at:
                up = jnp.where(live, up, 0.0)
            push[at : at + n, :] = up.astype(BF16)

    @pl.when(pl.program_id(0) < pl.num_programs(0) // 2)
    def _():
        fill(query_a, push_a)

    @pl.when(pl.program_id(0) >= pl.num_programs(0) // 2)
    def _():
        fill(query_b, push_b)


def attend_kernel(
    first, spot, lengths, query, push, key_a, key_b, value_a, value_b, low_a, low_b,
    r_key, r_value, r_low, low_t, lowered_t,
    q_up, kv_up, out_down, p_cos, p_sin, r_cos, r_sin, cos_t, sin_t, *others,
):
    if not first:
        fold_q_in, lifted_in, fold_kv_in, _, _ = others[:5]
        others = others[5:]
    (
        p_context, r_context, tiles, fold_q, lifted, fold_kv, fold_send, fold_reply,
        dk_t, dv_t, raw_q, mixed, keys, values, lows, bias,
    ) = others
    pr = p_context.shape[1]
    rl = r_context.shape[2]
    prompt = bias.shape[1]
    scale = HEAD_DIM ** (-0.5)
    step = scale * LOG2E
    heads = key_a.shape[1] // HEAD_DIM
    wide = query.shape[1] // heads
    share = wide // HEAD_DIM
    block = 512

    me = spot[0]
    places = []
    for other in (0, 1):
        for j in range(8):
            away, far = j // 2, j % 2
            z = jnp.bitwise_xor(me >> 3, far)
            y = jnp.bitwise_and((me >> 1) - away + 4, 3)
            c = jnp.bitwise_xor(jnp.bitwise_and(me, 1), other)
            places.append((other, j, pl.ds(pl.multiple_of((z * 8 + y * 2 + c) * pr, pr), pr)))

    row = lax.broadcasted_iota(jnp.int32, (pr, prompt), 0) + spot[0] * pr
    col = lax.broadcasted_iota(jnp.int32, (pr, prompt), 1)
    bias[...] = jnp.where(col <= row, 0.0, -jnp.inf)
    for other, j, rows in places:
        part = slice(j * pr, (j + 1) * pr)
        lows[rows, :] = (low_a, low_b)[other][part, :]
        for g in range(heads):
            cols = slice(g * HEAD_DIM, (g + 1) * HEAD_DIM)
            keys[g, rows, :] = (key_a, key_b)[other][part, cols]
            values[g, rows, :HEAD_DIM] = (value_a, value_b)[other][part, cols]
    lows[prompt:, :] = r_low[...]
    for g in range(heads):
        cols = slice(g * HEAD_DIM, (g + 1) * HEAD_DIM)
        keys[g, prompt:, :] = r_key[:, cols]
        values[g, prompt:, :HEAD_DIM] = r_value[:, cols]
        values[g, :, HEAD_DIM:] = jnp.ones((prompt + rl, HEAD_DIM), BF16)
    dk_t[...] = jnp.zeros_like(dk_t)
    dv_t[...] = jnp.zeros_like(dv_t)

    def stages(g, n, at, of, mask, keep, cos, sin, count):
        def stack(ref):
            return jnp.concatenate(
                [ref[at : at + n, h * HEAD_DIM : (h + 1) * HEAD_DIM] for h in of], axis=0
            )

        box = {}

        def scores():
            box["q"], box["p"] = stack(query), stack(push)
            box["score"] = mask(mm(box["q"], keys[g, :count, :], NT))

        def softmax():
            score = box.pop("score")
            top = jnp.max(score, axis=1, keepdims=True) * step
            box["weight"] = jnp.exp2(score * step - top).astype(BF16)

        def mix():
            box["summed"] = mm(box["weight"], values[g, :count, :])
            box["dprob"] = mm(box["p"], values[g, :count, :HEAD_DIM], NT)

        def backward():
            summed = box.pop("summed")
            share_of = 1.0 / summed[:, HEAD_DIM:]
            p = box.pop("p").astype(F32)
            context = keep((summed[:, :HEAD_DIM] * share_of).astype(BF16))
            delta = jnp.sum(context.astype(F32) * p, axis=1, keepdims=True)
            box["dscore"] = (box["weight"].astype(F32) * (box.pop("dprob") - delta)).astype(BF16)
            box["inverse"] = share_of * scale
            box["ps"] = (p * share_of).astype(BF16)
            box["qs"] = (box.pop("q").astype(F32) * box["inverse"]).astype(BF16)
            for i, h in enumerate(of):
                part = slice(i * n, (i + 1) * n)
                mixed[at : at + n, h * HEAD_DIM : (h + 1) * HEAD_DIM] = context[part]

        def products():
            dscore = box.pop("dscore")
            dv_t[g, :, :count] += mm(box.pop("ps"), box.pop("weight"), TN)
            dq = mm(dscore, keys[g, :count, :]) * box.pop("inverse")
            dk_t[g, :, :count] += mm(box.pop("qs"), dscore, TN)
            for i, h in enumerate(of):
                part = slice(i * n, (i + 1) * n)
                raw_q[at : at + n, h * HEAD_DIM : (h + 1) * HEAD_DIM] = unrope(
                    dq[part], cos[...], sin[...]
                ).astype(BF16)

        return scores, softmax, mix, backward, products

    p_heads = block // pr
    r_heads = block // rl

    def p_mask(score):
        seen = bias[...]
        return jnp.concatenate(
            [score[i * pr : (i + 1) * pr] + seen for i in range(p_heads)], axis=0
        )

    r_row = lax.broadcasted_iota(jnp.int32, (rl, rl), 0)
    r_col = lax.broadcasted_iota(jnp.int32, (rl, rl), 1)
    r_seen = jnp.concatenate([r_col <= r_row] * r_heads, axis=0)
    live = jnp.concatenate([r_row < lengths[0, 0]] * r_heads, axis=0)

    def r_mask(score):
        own = jnp.where(r_seen, score[:, prompt:], -jnp.inf)
        return jnp.concatenate([score[:, :prompt], own], axis=1)

    def finish(g):
        cols = slice(g * wide, (g + 1) * wide)
        context = mixed[:, cols]
        raw = raw_q[:, cols]
        p_context[0, :, cols] = mixed[:pr, cols]
        r_context[0, 0, :, cols] = mixed[pr:, cols]
        gq = (2.0 * mm(low_t[:RANK, :], raw)).astype(BF16)
        both = mm(lowered_t[...], context)
        god = (2.0 * (both[:RANK] + both[RANK:])).astype(BF16)
        first_tile = g * (2 * share + 2)
        for t in range(share):
            at = slice(t * HEAD_DIM, (t + 1) * HEAD_DIM)
            tiles[first_tile + t] = gq[:, at]
            tiles[first_tile + share + t] = god[:, at]
        upper, lower = dk_t[g, :HALF, :], dk_t[g, HALF:, :]
        cos, sin = cos_t[...], sin_t[...]
        raw_k = jnp.concatenate(
            [(upper * cos + lower * sin).astype(BF16), (lower * cos - upper * sin).astype(BF16)],
            axis=0,
        )
        raw_v = dv_t[g].astype(BF16)
        head = slice(g * HEAD_DIM, (g + 1) * HEAD_DIM)
        gk = jnp.transpose(mm(raw_k, lows[...]))
        gv = jnp.transpose(mm(raw_v, lows[...]))
        tiles[first_tile + 2 * share] = (2.0 * gk[RANK : 2 * RANK]).astype(BF16)
        tiles[first_tile + 2 * share + 1] = (2.0 * gv[2 * RANK : 3 * RANK]).astype(BF16)
        return (
            mm(q_up[:, cols], raw, NT),
            mm(out_down[:, cols], context, NT),
            mm(kv_up[0, :, head], raw_k),
            mm(kv_up[1, :, head], raw_v),
        )

    blocks = []
    for g in range(heads):
        for b in range(share // p_heads):
            of = [g * share + b * p_heads + i for i in range(p_heads)]
            blocks.append(stages(g, pr, 0, of, p_mask, lambda c: c, p_cos, p_sin, prompt))
        for b in range(share // r_heads):
            of = [g * share + b * r_heads + i for i in range(r_heads)]
            blocks.append(
                stages(
                    g, rl, pr, of, r_mask, lambda c: jnp.where(live, c, jnp.zeros_like(c)),
                    r_cos, r_sin, prompt + rl,
                )
            )
    each = len(blocks) // heads
    if first:
        folds = None
    else:
        folds = [fold_q_in[...], lifted_in[...], fold_kv_in[:RANK, :], fold_kv_in[RANK:, :]]
    for at in range(len(blocks) + 1):
        if at < len(blocks):
            blocks[at][0]()
        if at:
            blocks[at - 1][3]()
        if at < len(blocks):
            blocks[at][1]()
        if at:
            blocks[at - 1][4]()
        if at < len(blocks):
            blocks[at][2]()
        if at and at % each == 0:
            new = finish(at // each - 1)
            folds = new if folds is None else [x + y for x, y in zip(folds, new)]
    fold_q[...] = folds[0]
    lifted[...] = folds[1]
    fk, fv = folds[2], folds[3]
    fold_kv[:RANK, :] = fk
    fold_kv[RANK:, :] = fv
    for r in range(prompt // pr):
        cols = slice(r * pr, (r + 1) * pr)
        fold_send[r] = jnp.concatenate([fk[:, cols], fv[:, cols]], axis=1).astype(BF16)
    fold_reply[...] = jnp.concatenate([fk[:, prompt:], fv[:, prompt:]], axis=0).astype(BF16)


def grads_kernel(
    spot, fold_q, lifted, fold_reply, fold_recv, p_hidden, r_hidden, p_out, r_out, tiles_a, tiles_b,
    keep, give, held,
):
    pr = p_hidden.shape[1]
    fq = fold_q[...].astype(BF16)
    up = lifted[...].astype(BF16)
    own = jnp.sum(fold_recv[...].astype(F32), axis=0).astype(BF16)
    fp = jnp.concatenate([fq[:, :pr], own[:, :pr], own[:, pr:]], axis=0)
    fr = jnp.concatenate([fq[:, pr:], fold_reply[...]], axis=0)
    wide = p_hidden.shape[2] // HEAD_DIM
    down = (2.0 * (mm(fp, p_hidden[0]) + mm(fr, r_hidden[0, 0]))).astype(BF16)
    grad_up = (2.0 * (mm(up[:, :pr], p_out[0]) + mm(up[:, pr:], r_out[0, 0]))).astype(BF16)
    for t in range(wide):
        cols = slice(t * HEAD_DIM, (t + 1) * HEAD_DIM)
        for j in range(3):
            held[j * wide + t] = down[j * RANK : (j + 1) * RANK, cols]
        held[3 * wide + t] = grad_up[:, cols]
    at = 4 * wide
    small = tiles_a.shape[0]
    held[at : at + small] = tiles_a[...]
    held[at + small : at + 2 * small] = tiles_b[...]
    left = held.shape[0] - at - 2 * small
    held[at + 2 * small :] = jnp.zeros((left, RANK, HEAD_DIM), BF16)
    half = held.shape[0] // 2
    core = jnp.bitwise_and(spot[0], 1)

    @pl.when(core == 0)
    def _():
        keep[...] = held[:half]
        give[...] = held[half:]

    @pl.when(core == 1)
    def _():
        keep[...] = held[half:]
        give[...] = held[:half]


def unpack_kernel(spot, mine, theirs, down, gq, gkv, god, up, held):
    half = mine.shape[0]
    core = jnp.bitwise_and(spot[0], 1)

    @pl.when(core == 0)
    def _():
        held[:half] = mine[...]
        held[half:] = theirs[...]

    @pl.when(core == 1)
    def _():
        held[half:] = mine[...]
        held[:half] = theirs[...]

    def cols(t):
        return slice(t * HEAD_DIM, (t + 1) * HEAD_DIM)

    wide = down.shape[1] // HEAD_DIM
    for t in range(wide):
        for j in range(3):
            down[j * RANK : (j + 1) * RANK, cols(t)] = held[j * wide + t].astype(F32)
        up[:, cols(t)] = held[3 * wide + t].astype(F32)
    at = 4 * wide
    heads = gkv.shape[1] // HEAD_DIM
    share = gq.shape[1] // HEAD_DIM // heads
    for g in range(heads):
        for t in range(share):
            gq[:, cols(g * share + t)] = held[at + t].astype(F32)
            god[:, cols(g * share + t)] = held[at + share + t].astype(F32)
        gkv[:RANK, cols(g)] = held[at + 2 * share].astype(F32)
        gkv[RANK:, cols(g)] = held[at + 2 * share + 1].astype(F32)
        at += 2 * share + 2


def whole(shape):
    return pl.BlockSpec(shape, lambda *_: (0,) * len(shape))


def shifted(x, axis, by):
    n = lax.axis_size(axis)
    return lax.ppermute(x, axis, [(i, (i + by) % n) for i in range(n)])


def chips_of(pair):
    return [pair] + [shifted(pair, "y", k) for k in (1, 2, 3)]


def per_device(
    prompt_hidden,
    prompt_base,
    reply_hidden,
    reply_base,
    reply_lengths,
    adapter_down,
    query_up_weight,
    key_value_up_weight,
    output_down,
    output_up,
    prompt_grad_out,
    prompt_grad_base,
    reply_grad_out,
    reply_grad_base,
):
    group = lax.axis_size(RESP)
    pr = prompt_hidden.shape[1]
    rl = reply_hidden.shape[2]
    d = prompt_hidden.shape[2]
    prompt = pr * group
    q_width = query_up_weight.shape[1]
    kv_width = key_value_up_weight.shape[2]
    heads = kv_width // HEAD_DIM
    each = heads // 2
    qb = q_width // heads
    share = qb // HEAD_DIM
    rows = pr + rl
    wide = 2 * kv_width + HEAD_DIM
    low_at = 2 * kv_width // HEAD_DIM

    spot = lax.axis_index(RESP).astype(jnp.int32)[None]
    down = jnp.transpose(adapter_down, (0, 2, 1)).reshape(3 * RANK, d)
    out_down = jnp.transpose(output_down)
    cos, sin = rope_tables(prompt + rl)
    cos_rows = jnp.asarray(np.concatenate([cos, cos], axis=1), F32)
    sin_rows = jnp.asarray(np.concatenate([-sin, sin], axis=1), F32)
    cos_t = jnp.asarray(cos.T, F32)
    sin_t = jnp.asarray(sin.T, F32)
    p_table = pl.BlockSpec((pr, HEAD_DIM), lambda i, s: (s[0], 0))
    r_table = pl.BlockSpec((rl, HEAD_DIM), lambda i, *_: (prompt // rl, 0))

    own_kv = pl.pallas_call(
        front_kernel,
        grid_spec=pltpu.PrefetchScalarGridSpec(
            num_scalar_prefetch=1,
            grid=(1,),
            in_specs=[
                whole((1, pr, d)),
                pl.BlockSpec((1, pr, 2 * kv_width), lambda i, s: (0, 0, q_width // (2 * kv_width))),
                whole((3 * RANK, d)),
                whole((2, RANK, kv_width)),
                p_table,
                p_table,
            ],
            out_specs=whole((pr, wide)),
        ),
        out_shape=jax.ShapeDtypeStruct((pr, wide), BF16),
        name="front",
        **params(2 * pr * d * 48, 2_000_000, 56),
    )(spot, prompt_hidden, prompt_base, down, key_value_up_weight, cos_rows, sin_rows)

    far_kv = lax.ppermute(own_kv, "z_lo", PAIR)

    reply_kv, lows, splits, low_t, lowered_t = pl.pallas_call(
        reply_kernel,
        grid=(1,),
        in_specs=[
            pl.BlockSpec(memory_space=pltpu.SMEM),
            pl.BlockSpec((pr, HEAD_DIM), lambda i: (0, kv_width // HEAD_DIM)),
            whole((1, pr, d)),
            whole((1, 1, rl, d)),
            pl.BlockSpec(
                (1, 1, rl, 2 * kv_width), lambda i: (0, 0, 0, q_width // (2 * kv_width))
            ),
            whole((1, 1, rl, d)),
            whole((3 * RANK, d)),
            whole((2, RANK, kv_width)),
            whole((RANK, d)),
            r_table,
            r_table,
        ],
        out_specs=[
            whole((rl, wide)),
            whole((rows, HEAD_DIM)),
            whole((rows, HEAD_DIM)),
            whole((3 * RANK, rows)),
            whole((2 * RANK, rows)),
        ],
        out_shape=[
            jax.ShapeDtypeStruct((rl, wide), BF16),
            jax.ShapeDtypeStruct((rows, HEAD_DIM), BF16),
            jax.ShapeDtypeStruct((rows, HEAD_DIM), BF16),
            jax.ShapeDtypeStruct((3 * RANK, rows), BF16),
            jax.ShapeDtypeStruct((2 * RANK, rows), BF16),
        ],
        name="reply",
        **params(4 * rows * d * 48, 6_000_000, 56),
    )(
        reply_lengths, own_kv, prompt_grad_out, reply_hidden, reply_base, reply_grad_out, down,
        key_value_up_weight, output_up, cos_rows, sin_rows,
    )

    own_kv, far_kv, lows, splits = lax.optimization_barrier((own_kv, far_kv, lows, splits))
    cut = kv_width + HEAD_DIM
    first_pair = jnp.concatenate([own_kv[:, :cut], far_kv[:, :cut]], axis=0)
    second_pair = jnp.concatenate([own_kv[:, cut:], far_kv[:, cut:]], axis=0)
    first_parts = chips_of(first_pair)

    def head_cols(n, width, shift=0):
        return pl.BlockSpec((n, width), lambda i, s: (0, i + shift))

    def cols3(shift=0):
        return pl.BlockSpec((1, pr, qb), lambda i, s: (0, 0, i + shift))

    def cols4(shift=0):
        return pl.BlockSpec((1, 1, rl, qb), lambda i, s: (0, 0, 0, i + shift))

    query_a, push_a, query_b, push_b, mark = pl.pallas_call(
        query_kernel,
        grid_spec=pltpu.PrefetchScalarGridSpec(
            num_scalar_prefetch=1,
            grid=(heads,),
            in_specs=[
                pl.BlockSpec(memory_space=pltpu.SMEM),
                whole((rows, HEAD_DIM)),
                whole((rows, HEAD_DIM)),
                cols3(),
                cols3(),
                cols4(),
                cols4(),
                head_cols(RANK, qb),
                head_cols(RANK, qb),
                p_table,
                p_table,
                r_table,
                r_table,
            ],
            out_specs=[
                pl.BlockSpec((rows, qb), lambda i, s: (0, jnp.minimum(i, each - 1))),
                pl.BlockSpec((rows, qb), lambda i, s: (0, jnp.minimum(i, each - 1))),
                pl.BlockSpec((rows, qb), lambda i, s: (0, jnp.maximum(i - each, 0))),
                pl.BlockSpec((rows, qb), lambda i, s: (0, jnp.maximum(i - each, 0))),
                whole((RANK, HEAD_DIM)),
            ],
        ),
        out_shape=[
            jax.ShapeDtypeStruct((rows, q_width // 2), BF16),
            jax.ShapeDtypeStruct((rows, q_width // 2), BF16),
            jax.ShapeDtypeStruct((rows, q_width // 2), BF16),
            jax.ShapeDtypeStruct((rows, q_width // 2), BF16),
            jax.ShapeDtypeStruct((RANK, HEAD_DIM), BF16),
        ],
        name="query",
        **params(4 * rows * q_width * 128, 8_000_000, 48),
    )(
        spot, reply_lengths, lows, splits, prompt_base, prompt_grad_base, reply_base,
        reply_grad_base, query_up_weight, out_down, cos_rows, sin_rows, cos_rows, sin_rows,
    )

    first_parts, second_pair, query_a, push_a = lax.optimization_barrier(
        (first_parts, second_pair, query_a, push_a)
    )
    first_own = jnp.concatenate(first_parts, axis=0)
    first_other = lax.ppermute(first_own, "core", PAIR)
    second_parts = chips_of(second_pair)
    count = prompt // 2
    low_block = pl.BlockSpec((count, HEAD_DIM), lambda i, s: (0, kv_width // HEAD_DIM))

    def attend(query, push, own, other, at, before):
        first = before is None
        kb = each * HEAD_DIM
        in_specs = [
            pl.BlockSpec(memory_space=pltpu.SMEM),
            whole((rows, each * qb)),
            whole((rows, each * qb)),
            head_cols(count, kb),
            head_cols(count, kb),
            head_cols(count, kb, 1),
            head_cols(count, kb, 1),
            low_block,
            low_block,
            head_cols(rl, kb, at),
            head_cols(rl, kb, heads // each + at),
            pl.BlockSpec((rl, HEAD_DIM), lambda i, s: (0, low_at)),
            whole((3 * RANK, rows)),
            whole((2 * RANK, rows)),
            head_cols(RANK, each * qb, at),
            pl.BlockSpec((2, RANK, kb), lambda i, s: (0, 0, i + at)),
            head_cols(RANK, each * qb, at),
            p_table,
            p_table,
            r_table,
            r_table,
            whole((HALF, prompt + rl)),
            whole((HALF, prompt + rl)),
        ]
        operands = [
            spot, reply_lengths, query, push, own, other, own, other, first_own, first_other,
            reply_kv, reply_kv, reply_kv, low_t, lowered_t, query_up_weight, key_value_up_weight,
            out_down, cos_rows, sin_rows, cos_rows, sin_rows, cos_t, sin_t,
        ]
        aliases = {}
        if not first:
            aliases = {len(operands) + 3: 0, len(operands) + 4: 1}
            in_specs += [
                whole((RANK, rows)),
                whole((RANK, rows)),
                whole((2 * RANK, prompt + rl)),
                pl.BlockSpec(memory_space=pl.ANY),
                pl.BlockSpec(memory_space=pl.ANY),
            ]
            operands += list(before)
        per_head = 2 * share + 2
        return pl.pallas_call(
            functools.partial(attend_kernel, first),
            grid_spec=pltpu.PrefetchScalarGridSpec(
                num_scalar_prefetch=1,
                grid=(1,),
                in_specs=in_specs,
                out_specs=[
                    pl.BlockSpec((1, pr, each * qb), lambda i, s: (0, 0, i + at)),
                    pl.BlockSpec((1, 1, rl, each * qb), lambda i, s: (0, 0, 0, i + at)),
                    whole((each * per_head, RANK, HEAD_DIM)),
                    whole((RANK, rows)),
                    whole((RANK, rows)),
                    whole((2 * RANK, prompt + rl)),
                    whole((group, RANK, 2 * pr)),
                    whole((2 * RANK, rl)),
                ],
                scratch_shapes=[
                    pltpu.VMEM((each, HEAD_DIM, prompt + rl), F32),
                    pltpu.VMEM((each, HEAD_DIM, prompt + rl), F32),
                    pltpu.VMEM((rows, each * qb), BF16),
                    pltpu.VMEM((rows, each * qb), BF16),
                    pltpu.VMEM((each, prompt + rl, HEAD_DIM), BF16),
                    pltpu.VMEM((each, prompt + rl, 2 * HEAD_DIM), BF16),
                    pltpu.VMEM((prompt + rl, HEAD_DIM), BF16),
                    pltpu.VMEM((pr, prompt), F32),
                ],
            ),
            out_shape=[
                jax.ShapeDtypeStruct((1, pr, q_width), BF16),
                jax.ShapeDtypeStruct((1, 1, rl, q_width), BF16),
                jax.ShapeDtypeStruct((each * per_head, RANK, HEAD_DIM), BF16),
                jax.ShapeDtypeStruct((RANK, rows), F32),
                jax.ShapeDtypeStruct((RANK, rows), F32),
                jax.ShapeDtypeStruct((2 * RANK, prompt + rl), F32),
                jax.ShapeDtypeStruct((group, RANK, 2 * pr), BF16),
                jax.ShapeDtypeStruct((2 * RANK, rl), BF16),
            ],
            input_output_aliases=aliases,
            name="attend",
            **params(12 * rows * prompt * q_width // 2, 8_000_000),
        )(*operands)

    p_half, r_half, tiles_a, fold_q, lifted, fold_kv, _, _ = attend(
        query_a, push_a, first_own, first_other, 0, None
    )
    second_parts, fold_q, lifted, fold_kv = lax.optimization_barrier(
        (second_parts, fold_q, lifted, fold_kv)
    )
    second_own = jnp.concatenate(second_parts, axis=0)
    second_other = lax.ppermute(second_own, "core", PAIR)
    p_context, r_context, tiles_b, fold_q, lifted, _, fold_send, fold_reply = attend(
        query_b, push_b, second_own, second_other, 1, (fold_q, lifted, fold_kv, p_half, r_half)
    )

    fold_recv = lax.all_to_all(fold_send, RESP, 0, 0, tiled=True)

    slots = 2 * lax.axis_size(CHIPS) * 2
    half = slots // 2
    keep, give = pl.pallas_call(
        grads_kernel,
        grid_spec=pltpu.PrefetchScalarGridSpec(
            num_scalar_prefetch=1,
            grid=(1,),
            in_specs=[
                whole((RANK, rows)),
                whole((RANK, rows)),
                whole((2 * RANK, rl)),
                whole((group, RANK, 2 * pr)),
                whole((1, pr, d)),
                whole((1, 1, rl, d)),
                whole((1, pr, d)),
                whole((1, 1, rl, d)),
                whole(tiles_a.shape),
                whole(tiles_b.shape),
            ],
            out_specs=[whole((half, RANK, HEAD_DIM)), whole((half, RANK, HEAD_DIM))],
            scratch_shapes=[pltpu.VMEM((slots, RANK, HEAD_DIM), BF16)],
        ),
        out_shape=[jax.ShapeDtypeStruct((half, RANK, HEAD_DIM), BF16)] * 2,
        name="grads",
        **params(2 * rows * d * 64, 5_000_000),
    )(
        spot, fold_q, lifted, fold_reply, fold_recv, prompt_hidden, reply_hidden, prompt_grad_out,
        reply_grad_out, tiles_a, tiles_b,
    )

    chips = lax.axis_size(CHIPS)
    got = lax.ppermute(give, "core", PAIR)
    paired = (keep.astype(F32) + got.astype(F32)).astype(BF16)
    spread = lax.all_to_all(
        paired.reshape(chips, -1, HEAD_DIM), CHIPS, 0, 0, tiled=True
    )
    total = jnp.sum(spread.astype(F32), axis=0).astype(BF16)
    mine = lax.all_to_all(
        jnp.broadcast_to(total[None], spread.shape), CHIPS, 0, 0, tiled=True
    ).reshape(half, RANK, HEAD_DIM)
    theirs = lax.ppermute(mine, "core", PAIR)

    shapes = [(3 * RANK, d), (RANK, q_width), (2 * RANK, kv_width), (RANK, q_width), (RANK, d)]
    sum_down, sum_q, sum_kv, sum_od, sum_up = pl.pallas_call(
        unpack_kernel,
        grid_spec=pltpu.PrefetchScalarGridSpec(
            num_scalar_prefetch=1,
            grid=(1,),
            in_specs=[whole((half, RANK, HEAD_DIM))] * 2,
            out_specs=[whole(x) for x in shapes],
            scratch_shapes=[pltpu.VMEM((slots, RANK, HEAD_DIM), BF16)],
        ),
        out_shape=[jax.ShapeDtypeStruct(x, F32) for x in shapes],
        name="unpack",
        **params(0, 3_000_000),
    )(spot, mine, theirs)
    return (
        p_context,
        r_context,
        jnp.transpose(sum_down.reshape(3, RANK, d), (0, 2, 1)),
        sum_q,
        sum_kv.reshape(2, RANK, kv_width),
        jnp.transpose(sum_od),
        sum_up,
    )


def solution(mesh):
    fine = Mesh(mesh.devices.reshape(SIZES), CTX + RESP)
    return jax.shard_map(
        per_device,
        mesh=fine,
        in_specs=(
            P(CTX, RESP, None),
            P(CTX, RESP, None),
            P(CTX, RESP, None, None),
            P(CTX, RESP, None, None),
            P(CTX, RESP),
            P(),
            P(),
            P(),
            P(),
            P(),
            P(CTX, RESP, None),
            P(CTX, RESP, None),
            P(CTX, RESP, None, None),
            P(CTX, RESP, None, None),
        ),
        out_specs=(P(CTX, RESP, None), P(CTX, RESP, None, None), P(), P(), P(), P(), P()),
        check_vma=False,
    )
```

```python
import functools

import jax
import jax.numpy as jnp
import numpy as np
from jax import lax
from jax.experimental import pallas as pl
from jax.experimental.pallas import tpu as pltpu
from jax.sharding import Mesh
from jax.sharding import PartitionSpec as P

HEAD_DIM = 128
HALF = 64
RANK = 16
ROPE_BASE = 1000000.0
LOG2E = 1.4426950408889634
F32 = jnp.float32
BF16 = jnp.bfloat16
CTX = ("x", "z_hi")
RESP = ("z_lo", "y", "core")
CHIPS = ("x", "z_hi", "z_lo", "y")
SIZES = (4, 2, 2, 4, 2)
PAIR = [(0, 1), (1, 0)]

NN = (((1,), (0,)), ((), ()))
NT = (((1,), (1,)), ((), ()))
TN = (((0,), (0,)), ((), ()))


def mm(a, b, dims=NN):
    return lax.dot_general(a, b, dims, preferred_element_type=F32)


def rope_tables(count):
    rates = ROPE_BASE ** (-(np.arange(HALF, dtype=np.float64) * (2.0 / HEAD_DIM)))
    angle = np.arange(count, dtype=np.float64)[:, None] * rates[None, :]
    return np.cos(angle), np.sin(angle)


def rope(x, cos, sin):
    return x * cos + pltpu.roll(x, HALF, 1) * sin


def unrope(x, cos, sin):
    return x * cos - pltpu.roll(x, HALF, 1) * sin


def params(flops=0, nbytes=0, mib=36):
    return dict(
        compiler_params=pltpu.CompilerParams(vmem_limit_bytes=mib * 1024 * 1024),
        cost_estimate=pl.CostEstimate(flops=flops, bytes_accessed=nbytes, transcendentals=0),
    )


def kv_rows(hidden, base, down, kv_up, cos, sin):
    kv_width = kv_up.shape[2]
    low = mm(hidden, down, NT).astype(BF16)
    zero = jnp.zeros((RANK, kv_width), BF16)
    k_lift = jnp.concatenate([zero, kv_up[0], zero], axis=0)
    v_lift = jnp.concatenate([zero, zero, kv_up[1]], axis=0)
    key = base[:, :kv_width].astype(F32) + 2.0 * mm(low, k_lift)
    value = base[:, kv_width:].astype(F32) + 2.0 * mm(low, v_lift)
    heads = [
        rope(key[:, h : h + HEAD_DIM], cos, sin).astype(BF16)
        for h in range(0, kv_width, HEAD_DIM)
    ]
    return low, jnp.concatenate(heads, axis=1), value.astype(BF16)


def pad_low(low):
    return jnp.concatenate([low, jnp.zeros((low.shape[0], HEAD_DIM - 3 * RANK), BF16)], axis=1)


def front_kernel(spot, hidden, base, down, kv_up, cos, sin, out):
    low, key, value = kv_rows(hidden[0], base[0], down[...], kv_up[...], cos[...], sin[...])
    half = key.shape[1] // 2
    out[...] = jnp.concatenate(
        [key[:, :half], value[:, :half], pad_low(low), key[:, half:], value[:, half:]], axis=1
    )


def reply_kernel(
    lengths, p_low, p_out, r_hidden, r_base, r_out, down, kv_up, out_up, r_cos, r_sin,
    r_kv, lows, splits, low_t, lowered_t,
):
    pr = p_low.shape[0]
    rl = r_hidden.shape[2]
    r_low, r_key, r_value = kv_rows(
        r_hidden[0, 0], r_base[0, 0], down[...], kv_up[...], r_cos[...], r_sin[...]
    )
    r_low = pad_low(r_low)
    r_kv[...] = jnp.concatenate([r_key, r_value, r_low], axis=1)
    live = lax.broadcasted_iota(jnp.int32, (rl, RANK), 0) < lengths[0, 0]
    p_lowered = mm(p_out[0], out_up[...], NT)
    r_lowered = jnp.where(live, mm(r_out[0, 0], out_up[...], NT), 0.0)
    for low, lowered, at, n in ((p_low[...], p_lowered, 0, pr), (r_low, r_lowered, pr, rl)):
        lows[at : at + n, :] = low
        low_t[:, pl.ds(at, n)] = jnp.transpose(low.astype(F32))[: 3 * RANK].astype(BF16)
        high = lowered.astype(BF16)
        lost = (lowered - high.astype(F32)).astype(BF16)
        zero = jnp.zeros((n, HEAD_DIM - 2 * RANK), BF16)
        both = jnp.concatenate([high, lost, zero], axis=1)
        splits[at : at + n, :] = both
        lowered_t[:, pl.ds(at, n)] = jnp.transpose(both.astype(F32))[: 2 * RANK].astype(BF16)


def query_kernel(
    spot, lengths, lows, splits, p_base, p_gbase, r_base, r_gbase, q_up, out_down,
    p_cos, p_sin, r_cos, r_sin, query_a, push_a, query_b, push_b, mark,
):
    mark[...] = splits[: mark.shape[0], :]
    pr = p_base.shape[1]
    rl = r_base.shape[2]
    wide = q_up.shape[1]
    live = lax.broadcasted_iota(jnp.int32, (rl, wide), 0) < lengths[0, 0]
    q_lift = jnp.concatenate([q_up[...], jnp.zeros((HEAD_DIM - RANK, wide), BF16)], axis=0)
    o_lift = jnp.concatenate(
        [out_down[...], out_down[...], jnp.zeros((HEAD_DIM - 2 * RANK, wide), BF16)], axis=0
    )
    def fill(query, push):
        for base, gbase, cos, sin, at, n in (
            (p_base[0], p_gbase[0], p_cos, p_sin, 0, pr),
            (r_base[0, 0], r_gbase[0, 0], r_cos, r_sin, pr, rl),
        ):
            q = base.astype(F32) + 2.0 * mm(lows[at : at + n, :], q_lift)
            for h in range(0, wide, HEAD_DIM):
                query[at : at + n, h : h + HEAD_DIM] = rope(
                    q[:, h : h + HEAD_DIM], cos[...], sin[...]
                ).astype(BF16)
            up = gbase.astype(F32) + 2.0 * mm(splits[at : at + n, :], o_lift)
            if at:
                up = jnp.where(live, up, 0.0)
            push[at : at + n, :] = up.astype(BF16)

    @pl.when(pl.program_id(0) < pl.num_programs(0) // 2)
    def _():
        fill(query_a, push_a)

    @pl.when(pl.program_id(0) >= pl.num_programs(0) // 2)
    def _():
        fill(query_b, push_b)


def attend_kernel(
    first, spot, lengths, query, push, key_a, key_b, value_a, value_b, low_a, low_b,
    r_key, r_value, r_low, low_t, lowered_t,
    q_up, kv_up, out_down, p_cos, p_sin, r_cos, r_sin, cos_t, sin_t, *others,
):
    if not first:
        fold_q_in, lifted_in, fold_kv_in, _, _ = others[:5]
        others = others[5:]
    (
        p_context, r_context, tiles, fold_q, lifted, fold_kv, fold_send, fold_reply,
        dk_t, dv_t, raw_q, mixed, keys, values, lows, bias,
    ) = others
    pr = p_context.shape[1]
    rl = r_context.shape[2]
    prompt = bias.shape[1]
    scale = HEAD_DIM ** (-0.5)
    step = scale * LOG2E
    heads = key_a.shape[1] // HEAD_DIM
    wide = query.shape[1] // heads
    share = wide // HEAD_DIM
    block = 512

    me = spot[0]
    places = []
    for other in (0, 1):
        for j in range(8):
            away, far = j // 2, j % 2
            z = jnp.bitwise_xor(me >> 3, far)
            y = jnp.bitwise_and((me >> 1) - away + 4, 3)
            c = jnp.bitwise_xor(jnp.bitwise_and(me, 1), other)
            places.append((other, j, pl.ds(pl.multiple_of((z * 8 + y * 2 + c) * pr, pr), pr)))

    row = lax.broadcasted_iota(jnp.int32, (pr, prompt), 0) + spot[0] * pr
    col = lax.broadcasted_iota(jnp.int32, (pr, prompt), 1)
    bias[...] = jnp.where(col <= row, 0.0, -jnp.inf)
    for other, j, rows in places:
        part = slice(j * pr, (j + 1) * pr)
        lows[rows, :] = (low_a, low_b)[other][part, :]
        for g in range(heads):
            cols = slice(g * HEAD_DIM, (g + 1) * HEAD_DIM)
            keys[g, rows, :] = (key_a, key_b)[other][part, cols]
            values[g, rows, :HEAD_DIM] = (value_a, value_b)[other][part, cols]
    lows[prompt:, :] = r_low[...]
    for g in range(heads):
        cols = slice(g * HEAD_DIM, (g + 1) * HEAD_DIM)
        keys[g, prompt:, :] = r_key[:, cols]
        values[g, prompt:, :HEAD_DIM] = r_value[:, cols]
        values[g, :, HEAD_DIM:] = jnp.ones((prompt + rl, HEAD_DIM), BF16)
    dk_t[...] = jnp.zeros_like(dk_t)
    dv_t[...] = jnp.zeros_like(dv_t)

    def stages(g, n, at, of, mask, keep, cos, sin, count):
        def stack(ref):
            return jnp.concatenate(
                [ref[at : at + n, h * HEAD_DIM : (h + 1) * HEAD_DIM] for h in of], axis=0
            )

        box = {}

        def scores():
            box["q"], box["p"] = stack(query), stack(push)
            box["score"] = mask(mm(box["q"], keys[g, :count, :], NT))

        def softmax():
            score = box.pop("score")
            top = jnp.max(score, axis=1, keepdims=True) * step
            box["weight"] = jnp.exp2(score * step - top).astype(BF16)

        def mix():
            box["summed"] = mm(box["weight"], values[g, :count, :])
            box["dprob"] = mm(box["p"], values[g, :count, :HEAD_DIM], NT)

        def backward():
            summed = box.pop("summed")
            share_of = 1.0 / summed[:, HEAD_DIM:]
            p = box.pop("p").astype(F32)
            context = keep((summed[:, :HEAD_DIM] * share_of).astype(BF16))
            delta = jnp.sum(context.astype(F32) * p, axis=1, keepdims=True)
            box["dscore"] = (box["weight"].astype(F32) * (box.pop("dprob") - delta)).astype(BF16)
            box["inverse"] = share_of * scale
            box["ps"] = (p * share_of).astype(BF16)
            box["qs"] = (box.pop("q").astype(F32) * box["inverse"]).astype(BF16)
            for i, h in enumerate(of):
                part = slice(i * n, (i + 1) * n)
                mixed[at : at + n, h * HEAD_DIM : (h + 1) * HEAD_DIM] = context[part]

        def products():
            dscore = box.pop("dscore")
            dv_t[g, :, :count] += mm(box.pop("ps"), box.pop("weight"), TN)
            dq = mm(dscore, keys[g, :count, :]) * box.pop("inverse")
            dk_t[g, :, :count] += mm(box.pop("qs"), dscore, TN)
            for i, h in enumerate(of):
                part = slice(i * n, (i + 1) * n)
                raw_q[at : at + n, h * HEAD_DIM : (h + 1) * HEAD_DIM] = unrope(
                    dq[part], cos[...], sin[...]
                ).astype(BF16)

        return scores, softmax, mix, backward, products

    p_heads = block // pr
    r_heads = block // rl

    def p_mask(score):
        seen = bias[...]
        return jnp.concatenate(
            [score[i * pr : (i + 1) * pr] + seen for i in range(p_heads)], axis=0
        )

    r_row = lax.broadcasted_iota(jnp.int32, (rl, rl), 0)
    r_col = lax.broadcasted_iota(jnp.int32, (rl, rl), 1)
    r_seen = jnp.concatenate([r_col <= r_row] * r_heads, axis=0)
    live = jnp.concatenate([r_row < lengths[0, 0]] * r_heads, axis=0)

    def r_mask(score):
        own = jnp.where(r_seen, score[:, prompt:], -jnp.inf)
        return jnp.concatenate([score[:, :prompt], own], axis=1)

    def finish(g):
        cols = slice(g * wide, (g + 1) * wide)
        context = mixed[:, cols]
        raw = raw_q[:, cols]
        p_context[0, :, cols] = mixed[:pr, cols]
        r_context[0, 0, :, cols] = mixed[pr:, cols]
        gq = (2.0 * mm(low_t[:RANK, :], raw)).astype(BF16)
        both = mm(lowered_t[...], context)
        god = (2.0 * (both[:RANK] + both[RANK:])).astype(BF16)
        first_tile = g * (2 * share + 2)
        for t in range(share):
            at = slice(t * HEAD_DIM, (t + 1) * HEAD_DIM)
            tiles[first_tile + t] = gq[:, at]
            tiles[first_tile + share + t] = god[:, at]
        upper, lower = dk_t[g, :HALF, :], dk_t[g, HALF:, :]
        cos, sin = cos_t[...], sin_t[...]
        raw_k = jnp.concatenate(
            [(upper * cos + lower * sin).astype(BF16), (lower * cos - upper * sin).astype(BF16)],
            axis=0,
        )
        raw_v = dv_t[g].astype(BF16)
        head = slice(g * HEAD_DIM, (g + 1) * HEAD_DIM)
        gk = jnp.transpose(mm(raw_k, lows[...]))
        gv = jnp.transpose(mm(raw_v, lows[...]))
        tiles[first_tile + 2 * share] = (2.0 * gk[RANK : 2 * RANK]).astype(BF16)
        tiles[first_tile + 2 * share + 1] = (2.0 * gv[2 * RANK : 3 * RANK]).astype(BF16)
        return (
            mm(q_up[:, cols], raw, NT),
            mm(out_down[:, cols], context, NT),
            mm(kv_up[0, :, head], raw_k),
            mm(kv_up[1, :, head], raw_v),
        )

    blocks = []
    for g in range(heads):
        for b in range(share // p_heads):
            of = [g * share + b * p_heads + i for i in range(p_heads)]
            blocks.append(stages(g, pr, 0, of, p_mask, lambda c: c, p_cos, p_sin, prompt))
        for b in range(share // r_heads):
            of = [g * share + b * r_heads + i for i in range(r_heads)]
            blocks.append(
                stages(
                    g, rl, pr, of, r_mask, lambda c: jnp.where(live, c, jnp.zeros_like(c)),
                    r_cos, r_sin, prompt + rl,
                )
            )
    each = len(blocks) // heads
    if first:
        folds = None
    else:
        folds = [fold_q_in[...], lifted_in[...], fold_kv_in[:RANK, :], fold_kv_in[RANK:, :]]
    for at in range(len(blocks) + 1):
        if at < len(blocks):
            blocks[at][0]()
        if at:
            blocks[at - 1][3]()
        if at < len(blocks):
            blocks[at][1]()
        if at:
            blocks[at - 1][4]()
        if at < len(blocks):
            blocks[at][2]()
        if at and at % each == 0:
            new = finish(at // each - 1)
            folds = new if folds is None else [x + y for x, y in zip(folds, new)]
    fold_q[...] = folds[0]
    lifted[...] = folds[1]
    fk, fv = folds[2], folds[3]
    fold_kv[:RANK, :] = fk
    fold_kv[RANK:, :] = fv
    for r in range(prompt // pr):
        cols = slice(r * pr, (r + 1) * pr)
        fold_send[r] = jnp.concatenate([fk[:, cols], fv[:, cols]], axis=1).astype(BF16)
    fold_reply[...] = jnp.concatenate([fk[:, prompt:], fv[:, prompt:]], axis=0).astype(BF16)


def grads_kernel(
    spot, fold_q, lifted, fold_reply, fold_recv, p_hidden, r_hidden, p_out, r_out, tiles_a, tiles_b,
    keep, give, held,
):
    pr = p_hidden.shape[1]
    fq = fold_q[...].astype(BF16)
    up = lifted[...].astype(BF16)
    own = jnp.sum(fold_recv[...].astype(F32), axis=0).astype(BF16)
    fp = jnp.concatenate([fq[:, :pr], own[:, :pr], own[:, pr:]], axis=0)
    fr = jnp.concatenate([fq[:, pr:], fold_reply[...]], axis=0)
    wide = p_hidden.shape[2] // HEAD_DIM
    down = (2.0 * (mm(fp, p_hidden[0]) + mm(fr, r_hidden[0, 0]))).astype(BF16)
    grad_up = (2.0 * (mm(up[:, :pr], p_out[0]) + mm(up[:, pr:], r_out[0, 0]))).astype(BF16)
    for t in range(wide):
        cols = slice(t * HEAD_DIM, (t + 1) * HEAD_DIM)
        for j in range(3):
            held[j * wide + t] = down[j * RANK : (j + 1) * RANK, cols]
        held[3 * wide + t] = grad_up[:, cols]
    at = 4 * wide
    small = tiles_a.shape[0]
    held[at : at + small] = tiles_a[...]
    held[at + small : at + 2 * small] = tiles_b[...]
    left = held.shape[0] - at - 2 * small
    held[at + 2 * small :] = jnp.zeros((left, RANK, HEAD_DIM), BF16)
    half = held.shape[0] // 2
    core = jnp.bitwise_and(spot[0], 1)

    @pl.when(core == 0)
    def _():
        keep[...] = held[:half]
        give[...] = held[half:]

    @pl.when(core == 1)
    def _():
        keep[...] = held[half:]
        give[...] = held[:half]


def unpack_kernel(spot, mine, theirs, down, gq, gkv, god, up, held):
    half = mine.shape[0]
    core = jnp.bitwise_and(spot[0], 1)

    @pl.when(core == 0)
    def _():
        held[:half] = mine[...]
        held[half:] = theirs[...]

    @pl.when(core == 1)
    def _():
        held[half:] = mine[...]
        held[:half] = theirs[...]

    def cols(t):
        return slice(t * HEAD_DIM, (t + 1) * HEAD_DIM)

    wide = down.shape[1] // HEAD_DIM
    for t in range(wide):
        for j in range(3):
            down[j * RANK : (j + 1) * RANK, cols(t)] = held[j * wide + t].astype(F32)
        up[:, cols(t)] = held[3 * wide + t].astype(F32)
    at = 4 * wide
    heads = gkv.shape[1] // HEAD_DIM
    share = gq.shape[1] // HEAD_DIM // heads
    for g in range(heads):
        for t in range(share):
            gq[:, cols(g * share + t)] = held[at + t].astype(F32)
            god[:, cols(g * share + t)] = held[at + share + t].astype(F32)
        gkv[:RANK, cols(g)] = held[at + 2 * share].astype(F32)
        gkv[RANK:, cols(g)] = held[at + 2 * share + 1].astype(F32)
        at += 2 * share + 2


def whole(shape):
    return pl.BlockSpec(shape, lambda *_: (0,) * len(shape))


def shifted(x, axis, by):
    n = lax.axis_size(axis)
    return lax.ppermute(x, axis, [(i, (i + by) % n) for i in range(n)])


def chips_of(pair, two):
    one, three = shifted(pair, "y", 1), shifted(pair, "y", 3)
    return [pair, one, two, lax.ppermute(two, "z_lo", PAIR), three]


def per_device(
    prompt_hidden,
    prompt_base,
    reply_hidden,
    reply_base,
    reply_lengths,
    adapter_down,
    query_up_weight,
    key_value_up_weight,
    output_down,
    output_up,
    prompt_grad_out,
    prompt_grad_base,
    reply_grad_out,
    reply_grad_base,
):
    group = lax.axis_size(RESP)
    pr = prompt_hidden.shape[1]
    rl = reply_hidden.shape[2]
    d = prompt_hidden.shape[2]
    prompt = pr * group
    q_width = query_up_weight.shape[1]
    kv_width = key_value_up_weight.shape[2]
    heads = kv_width // HEAD_DIM
    each = heads // 2
    qb = q_width // heads
    share = qb // HEAD_DIM
    rows = pr + rl
    wide = 2 * kv_width + HEAD_DIM
    low_at = 2 * kv_width // HEAD_DIM

    spot = lax.axis_index(RESP).astype(jnp.int32)[None]
    down = jnp.transpose(adapter_down, (0, 2, 1)).reshape(3 * RANK, d)
    out_down = jnp.transpose(output_down)
    cos, sin = rope_tables(prompt + rl)
    cos_rows = jnp.asarray(np.concatenate([cos, cos], axis=1), F32)
    sin_rows = jnp.asarray(np.concatenate([-sin, sin], axis=1), F32)
    cos_t = jnp.asarray(cos.T, F32)
    sin_t = jnp.asarray(sin.T, F32)
    p_table = pl.BlockSpec((pr, HEAD_DIM), lambda i, s: (s[0], 0))
    r_table = pl.BlockSpec((rl, HEAD_DIM), lambda i, *_: (prompt // rl, 0))

    own_kv = pl.pallas_call(
        front_kernel,
        grid_spec=pltpu.PrefetchScalarGridSpec(
            num_scalar_prefetch=1,
            grid=(1,),
            in_specs=[
                whole((1, pr, d)),
                pl.BlockSpec((1, pr, 2 * kv_width), lambda i, s: (0, 0, q_width // (2 * kv_width))),
                whole((3 * RANK, d)),
                whole((2, RANK, kv_width)),
                p_table,
                p_table,
            ],
            out_specs=whole((pr, wide)),
        ),
        out_shape=jax.ShapeDtypeStruct((pr, wide), BF16),
        name="front",
        **params(2 * pr * d * 48, 2_000_000, 56),
    )(spot, prompt_hidden, prompt_base, down, key_value_up_weight, cos_rows, sin_rows)

    far_kv = lax.ppermute(own_kv, "z_lo", PAIR)
    two_kv = shifted(own_kv, "y", 2)

    reply_kv, lows, splits, low_t, lowered_t = pl.pallas_call(
        reply_kernel,
        grid=(1,),
        in_specs=[
            pl.BlockSpec(memory_space=pltpu.SMEM),
            pl.BlockSpec((pr, HEAD_DIM), lambda i: (0, kv_width // HEAD_DIM)),
            whole((1, pr, d)),
            whole((1, 1, rl, d)),
            pl.BlockSpec(
                (1, 1, rl, 2 * kv_width), lambda i: (0, 0, 0, q_width // (2 * kv_width))
            ),
            whole((1, 1, rl, d)),
            whole((3 * RANK, d)),
            whole((2, RANK, kv_width)),
            whole((RANK, d)),
            r_table,
            r_table,
        ],
        out_specs=[
            whole((rl, wide)),
            whole((rows, HEAD_DIM)),
            whole((rows, HEAD_DIM)),
            whole((3 * RANK, rows)),
            whole((2 * RANK, rows)),
        ],
        out_shape=[
            jax.ShapeDtypeStruct((rl, wide), BF16),
            jax.ShapeDtypeStruct((rows, HEAD_DIM), BF16),
            jax.ShapeDtypeStruct((rows, HEAD_DIM), BF16),
            jax.ShapeDtypeStruct((3 * RANK, rows), BF16),
            jax.ShapeDtypeStruct((2 * RANK, rows), BF16),
        ],
        name="reply",
        **params(4 * rows * d * 48, 6_000_000, 56),
    )(
        reply_lengths, own_kv, prompt_grad_out, reply_hidden, reply_base, reply_grad_out, down,
        key_value_up_weight, output_up, cos_rows, sin_rows,
    )

    own_kv, far_kv, two_kv, lows, splits = lax.optimization_barrier(
        (own_kv, far_kv, two_kv, lows, splits)
    )
    cut = kv_width + HEAD_DIM
    parts = chips_of(jnp.concatenate([own_kv, far_kv], axis=0), two_kv)

    def head_cols(n, width, shift=0):
        return pl.BlockSpec((n, width), lambda i, s: (0, i + shift))

    def cols3(shift=0):
        return pl.BlockSpec((1, pr, qb), lambda i, s: (0, 0, i + shift))

    def cols4(shift=0):
        return pl.BlockSpec((1, 1, rl, qb), lambda i, s: (0, 0, 0, i + shift))

    query_a, push_a, query_b, push_b, mark = pl.pallas_call(
        query_kernel,
        grid_spec=pltpu.PrefetchScalarGridSpec(
            num_scalar_prefetch=1,
            grid=(heads,),
            in_specs=[
                pl.BlockSpec(memory_space=pltpu.SMEM),
                whole((rows, HEAD_DIM)),
                whole((rows, HEAD_DIM)),
                cols3(),
                cols3(),
                cols4(),
                cols4(),
                head_cols(RANK, qb),
                head_cols(RANK, qb),
                p_table,
                p_table,
                r_table,
                r_table,
            ],
            out_specs=[
                pl.BlockSpec((rows, qb), lambda i, s: (0, jnp.minimum(i, each - 1))),
                pl.BlockSpec((rows, qb), lambda i, s: (0, jnp.minimum(i, each - 1))),
                pl.BlockSpec((rows, qb), lambda i, s: (0, jnp.maximum(i - each, 0))),
                pl.BlockSpec((rows, qb), lambda i, s: (0, jnp.maximum(i - each, 0))),
                whole((RANK, HEAD_DIM)),
            ],
        ),
        out_shape=[
            jax.ShapeDtypeStruct((rows, q_width // 2), BF16),
            jax.ShapeDtypeStruct((rows, q_width // 2), BF16),
            jax.ShapeDtypeStruct((rows, q_width // 2), BF16),
            jax.ShapeDtypeStruct((rows, q_width // 2), BF16),
            jax.ShapeDtypeStruct((RANK, HEAD_DIM), BF16),
        ],
        name="query",
        **params(4 * rows * q_width * 128, 8_000_000, 48),
    )(
        spot, reply_lengths, lows, splits, prompt_base, prompt_grad_base, reply_base,
        reply_grad_base, query_up_weight, out_down, cos_rows, sin_rows, cos_rows, sin_rows,
    )

    parts, query_a, push_a = lax.optimization_barrier((parts, query_a, push_a))
    first_own = jnp.concatenate([x[:, :cut] for x in parts], axis=0)
    second_own = jnp.concatenate([x[:, cut:] for x in parts], axis=0)
    first_other = lax.ppermute(first_own, "core", PAIR)
    second_other = lax.ppermute(second_own, "core", PAIR)
    count = prompt // 2
    low_block = pl.BlockSpec((count, HEAD_DIM), lambda i, s: (0, kv_width // HEAD_DIM))

    def attend(query, push, own, other, at, before):
        first = before is None
        kb = each * HEAD_DIM
        in_specs = [
            pl.BlockSpec(memory_space=pltpu.SMEM),
            whole((rows, each * qb)),
            whole((rows, each * qb)),
            head_cols(count, kb),
            head_cols(count, kb),
            head_cols(count, kb, 1),
            head_cols(count, kb, 1),
            low_block,
            low_block,
            head_cols(rl, kb, at),
            head_cols(rl, kb, heads // each + at),
            pl.BlockSpec((rl, HEAD_DIM), lambda i, s: (0, low_at)),
            whole((3 * RANK, rows)),
            whole((2 * RANK, rows)),
            head_cols(RANK, each * qb, at),
            pl.BlockSpec((2, RANK, kb), lambda i, s: (0, 0, i + at)),
            head_cols(RANK, each * qb, at),
            p_table,
            p_table,
            r_table,
            r_table,
            whole((HALF, prompt + rl)),
            whole((HALF, prompt + rl)),
        ]
        operands = [
            spot, reply_lengths, query, push, own, other, own, other, first_own, first_other,
            reply_kv, reply_kv, reply_kv, low_t, lowered_t, query_up_weight, key_value_up_weight,
            out_down, cos_rows, sin_rows, cos_rows, sin_rows, cos_t, sin_t,
        ]
        aliases = {}
        if not first:
            aliases = {len(operands) + 3: 0, len(operands) + 4: 1}
            in_specs += [
                whole((RANK, rows)),
                whole((RANK, rows)),
                whole((2 * RANK, prompt + rl)),
                pl.BlockSpec(memory_space=pl.ANY),
                pl.BlockSpec(memory_space=pl.ANY),
            ]
            operands += list(before)
        per_head = 2 * share + 2
        return pl.pallas_call(
            functools.partial(attend_kernel, first),
            grid_spec=pltpu.PrefetchScalarGridSpec(
                num_scalar_prefetch=1,
                grid=(1,),
                in_specs=in_specs,
                out_specs=[
                    pl.BlockSpec((1, pr, each * qb), lambda i, s: (0, 0, i + at)),
                    pl.BlockSpec((1, 1, rl, each * qb), lambda i, s: (0, 0, 0, i + at)),
                    whole((each * per_head, RANK, HEAD_DIM)),
                    whole((RANK, rows)),
                    whole((RANK, rows)),
                    whole((2 * RANK, prompt + rl)),
                    whole((group, RANK, 2 * pr)),
                    whole((2 * RANK, rl)),
                ],
                scratch_shapes=[
                    pltpu.VMEM((each, HEAD_DIM, prompt + rl), F32),
                    pltpu.VMEM((each, HEAD_DIM, prompt + rl), F32),
                    pltpu.VMEM((rows, each * qb), BF16),
                    pltpu.VMEM((rows, each * qb), BF16),
                    pltpu.VMEM((each, prompt + rl, HEAD_DIM), BF16),
                    pltpu.VMEM((each, prompt + rl, 2 * HEAD_DIM), BF16),
                    pltpu.VMEM((prompt + rl, HEAD_DIM), BF16),
                    pltpu.VMEM((pr, prompt), F32),
                ],
            ),
            out_shape=[
                jax.ShapeDtypeStruct((1, pr, q_width), BF16),
                jax.ShapeDtypeStruct((1, 1, rl, q_width), BF16),
                jax.ShapeDtypeStruct((each * per_head, RANK, HEAD_DIM), BF16),
                jax.ShapeDtypeStruct((RANK, rows), F32),
                jax.ShapeDtypeStruct((RANK, rows), F32),
                jax.ShapeDtypeStruct((2 * RANK, prompt + rl), F32),
                jax.ShapeDtypeStruct((group, RANK, 2 * pr), BF16),
                jax.ShapeDtypeStruct((2 * RANK, rl), BF16),
            ],
            input_output_aliases=aliases,
            name="attend",
            **params(12 * rows * prompt * q_width // 2, 8_000_000),
        )(*operands)

    p_half, r_half, tiles_a, fold_q, lifted, fold_kv, _, _ = attend(
        query_a, push_a, first_own, first_other, 0, None
    )
    p_context, r_context, tiles_b, fold_q, lifted, _, fold_send, fold_reply = attend(
        query_b, push_b, second_own, second_other, 1, (fold_q, lifted, fold_kv, p_half, r_half)
    )

    fold_recv = lax.all_to_all(fold_send, RESP, 0, 0, tiled=True)

    slots = 2 * lax.axis_size(CHIPS) * 2
    half = slots // 2
    keep, give = pl.pallas_call(
        grads_kernel,
        grid_spec=pltpu.PrefetchScalarGridSpec(
            num_scalar_prefetch=1,
            grid=(1,),
            in_specs=[
                whole((RANK, rows)),
                whole((RANK, rows)),
                whole((2 * RANK, rl)),
                whole((group, RANK, 2 * pr)),
                whole((1, pr, d)),
                whole((1, 1, rl, d)),
                whole((1, pr, d)),
                whole((1, 1, rl, d)),
                whole(tiles_a.shape),
                whole(tiles_b.shape),
            ],
            out_specs=[whole((half, RANK, HEAD_DIM)), whole((half, RANK, HEAD_DIM))],
            scratch_shapes=[pltpu.VMEM((slots, RANK, HEAD_DIM), BF16)],
        ),
        out_shape=[jax.ShapeDtypeStruct((half, RANK, HEAD_DIM), BF16)] * 2,
        name="grads",
        **params(2 * rows * d * 64, 5_000_000),
    )(
        spot, fold_q, lifted, fold_reply, fold_recv, prompt_hidden, reply_hidden, prompt_grad_out,
        reply_grad_out, tiles_a, tiles_b,
    )

    chips = lax.axis_size(CHIPS)
    got = lax.ppermute(give, "core", PAIR)
    paired = (keep.astype(F32) + got.astype(F32)).astype(BF16)
    spread = lax.all_to_all(
        paired.reshape(chips, -1, HEAD_DIM), CHIPS, 0, 0, tiled=True
    )
    total = jnp.sum(spread.astype(F32), axis=0).astype(BF16)
    mine = lax.all_to_all(
        jnp.broadcast_to(total[None], spread.shape), CHIPS, 0, 0, tiled=True
    ).reshape(half, RANK, HEAD_DIM)
    theirs = lax.ppermute(mine, "core", PAIR)

    shapes = [(3 * RANK, d), (RANK, q_width), (2 * RANK, kv_width), (RANK, q_width), (RANK, d)]
    sum_down, sum_q, sum_kv, sum_od, sum_up = pl.pallas_call(
        unpack_kernel,
        grid_spec=pltpu.PrefetchScalarGridSpec(
            num_scalar_prefetch=1,
            grid=(1,),
            in_specs=[whole((half, RANK, HEAD_DIM))] * 2,
            out_specs=[whole(x) for x in shapes],
            scratch_shapes=[pltpu.VMEM((slots, RANK, HEAD_DIM), BF16)],
        ),
        out_shape=[jax.ShapeDtypeStruct(x, F32) for x in shapes],
        name="unpack",
        **params(0, 3_000_000),
    )(spot, mine, theirs)
    return (
        p_context,
        r_context,
        jnp.transpose(sum_down.reshape(3, RANK, d), (0, 2, 1)),
        sum_q,
        sum_kv.reshape(2, RANK, kv_width),
        jnp.transpose(sum_od),
        sum_up,
    )


def solution(mesh):
    fine = Mesh(mesh.devices.reshape(SIZES), CTX + RESP)
    return jax.shard_map(
        per_device,
        mesh=fine,
        in_specs=(
            P(CTX, RESP, None),
            P(CTX, RESP, None),
            P(CTX, RESP, None, None),
            P(CTX, RESP, None, None),
            P(CTX, RESP),
            P(),
            P(),
            P(),
            P(),
            P(),
            P(CTX, RESP, None),
            P(CTX, RESP, None),
            P(CTX, RESP, None, None),
            P(CTX, RESP, None, None),
        ),
        out_specs=(P(CTX, RESP, None), P(CTX, RESP, None, None), P(), P(), P(), P(), P()),
        check_vma=False,
    )
```

```python
import functools

import jax
import jax.numpy as jnp
import numpy as np
from jax import lax
from jax.experimental import pallas as pl
from jax.experimental.pallas import tpu as pltpu
from jax.sharding import Mesh
from jax.sharding import PartitionSpec as P

HEAD_DIM = 128
HALF = 64
RANK = 16
ROPE_BASE = 1000000.0
LOG2E = 1.4426950408889634
F32 = jnp.float32
BF16 = jnp.bfloat16
CTX = ("x", "z_hi")
RESP = ("z_lo", "y", "core")
CHIPS = ("x", "z_hi", "z_lo", "y")
SIZES = (4, 2, 2, 4, 2)
PAIR = [(0, 1), (1, 0)]

NN = (((1,), (0,)), ((), ()))
NT = (((1,), (1,)), ((), ()))
TN = (((0,), (0,)), ((), ()))


def mm(a, b, dims=NN):
    return lax.dot_general(a, b, dims, preferred_element_type=F32)


def rope_tables(count):
    rates = ROPE_BASE ** (-(np.arange(HALF, dtype=np.float64) * (2.0 / HEAD_DIM)))
    angle = np.arange(count, dtype=np.float64)[:, None] * rates[None, :]
    return np.cos(angle), np.sin(angle)


def rope(x, cos, sin):
    return x * cos + pltpu.roll(x, HALF, 1) * sin


def unrope(x, cos, sin):
    return x * cos - pltpu.roll(x, HALF, 1) * sin


def params(flops=0, nbytes=0, mib=36):
    return dict(
        compiler_params=pltpu.CompilerParams(vmem_limit_bytes=mib * 1024 * 1024),
        cost_estimate=pl.CostEstimate(flops=flops, bytes_accessed=nbytes, transcendentals=0),
    )


def kv_rows(hidden, base, down, kv_up, cos, sin):
    kv_width = kv_up.shape[2]
    low = mm(hidden, down, NT).astype(BF16)
    zero = jnp.zeros((RANK, kv_width), BF16)
    k_lift = jnp.concatenate([zero, kv_up[0], zero], axis=0)
    v_lift = jnp.concatenate([zero, zero, kv_up[1]], axis=0)
    key = base[:, :kv_width].astype(F32) + 2.0 * mm(low, k_lift)
    value = base[:, kv_width:].astype(F32) + 2.0 * mm(low, v_lift)
    heads = [
        rope(key[:, h : h + HEAD_DIM], cos, sin).astype(BF16)
        for h in range(0, kv_width, HEAD_DIM)
    ]
    return low, jnp.concatenate(heads, axis=1), value.astype(BF16)


def pad_low(low):
    return jnp.concatenate([low, jnp.zeros((low.shape[0], HEAD_DIM - 3 * RANK), BF16)], axis=1)


def front_kernel(spot, hidden, base, down, kv_up, cos, sin, out):
    low, key, value = kv_rows(hidden[0], base[0], down[...], kv_up[...], cos[...], sin[...])
    half = key.shape[1] // 2
    out[...] = jnp.concatenate(
        [key[:, :half], value[:, :half], pad_low(low), key[:, half:], value[:, half:]], axis=1
    )


def reply_kernel(
    lengths, p_low, p_out, r_hidden, r_base, r_out, down, kv_up, out_up, r_cos, r_sin,
    r_kv, lows, splits, low_t, lowered_t,
):
    pr = p_low.shape[0]
    rl = r_hidden.shape[2]
    r_low, r_key, r_value = kv_rows(
        r_hidden[0, 0], r_base[0, 0], down[...], kv_up[...], r_cos[...], r_sin[...]
    )
    r_low = pad_low(r_low)
    r_kv[...] = jnp.concatenate([r_key, r_value, r_low], axis=1)
    live = lax.broadcasted_iota(jnp.int32, (rl, RANK), 0) < lengths[0, 0]
    p_lowered = mm(p_out[0], out_up[...], NT)
    r_lowered = jnp.where(live, mm(r_out[0, 0], out_up[...], NT), 0.0)
    for low, lowered, at, n in ((p_low[...], p_lowered, 0, pr), (r_low, r_lowered, pr, rl)):
        lows[at : at + n, :] = low
        low_t[:, pl.ds(at, n)] = jnp.transpose(low.astype(F32))[: 3 * RANK].astype(BF16)
        high = lowered.astype(BF16)
        lost = (lowered - high.astype(F32)).astype(BF16)
        zero = jnp.zeros((n, HEAD_DIM - 2 * RANK), BF16)
        both = jnp.concatenate([high, lost, zero], axis=1)
        splits[at : at + n, :] = both
        lowered_t[:, pl.ds(at, n)] = jnp.transpose(both.astype(F32))[: 2 * RANK].astype(BF16)


def query_kernel(
    spot, lengths, lows, splits, p_base, p_gbase, r_base, r_gbase, q_up, out_down,
    p_cos, p_sin, r_cos, r_sin, query_a, push_a, query_b, push_b, mark,
):
    mark[...] = splits[: mark.shape[0], :]
    pr = p_base.shape[1]
    rl = r_base.shape[2]
    wide = q_up.shape[1]
    live = lax.broadcasted_iota(jnp.int32, (rl, wide), 0) < lengths[0, 0]
    q_lift = jnp.concatenate([q_up[...], jnp.zeros((HEAD_DIM - RANK, wide), BF16)], axis=0)
    o_lift = jnp.concatenate(
        [out_down[...], out_down[...], jnp.zeros((HEAD_DIM - 2 * RANK, wide), BF16)], axis=0
    )
    def fill(query, push):
        for base, gbase, cos, sin, at, n in (
            (p_base[0], p_gbase[0], p_cos, p_sin, 0, pr),
            (r_base[0, 0], r_gbase[0, 0], r_cos, r_sin, pr, rl),
        ):
            q = base.astype(F32) + 2.0 * mm(lows[at : at + n, :], q_lift)
            for h in range(0, wide, HEAD_DIM):
                query[at : at + n, h : h + HEAD_DIM] = rope(
                    q[:, h : h + HEAD_DIM], cos[...], sin[...]
                ).astype(BF16)
            up = gbase.astype(F32) + 2.0 * mm(splits[at : at + n, :], o_lift)
            if at:
                up = jnp.where(live, up, 0.0)
            push[at : at + n, :] = up.astype(BF16)

    @pl.when(pl.program_id(0) < pl.num_programs(0) // 2)
    def _():
        fill(query_a, push_a)

    @pl.when(pl.program_id(0) >= pl.num_programs(0) // 2)
    def _():
        fill(query_b, push_b)


def attend_kernel(
    first, spot, lengths, query, push, key_a, key_b, value_a, value_b, low_a, low_b,
    r_key, r_value, r_low, low_t, lowered_t,
    q_up, kv_up, out_down, p_cos, p_sin, r_cos, r_sin, cos_t, sin_t, *others,
):
    if not first:
        fold_q_in, lifted_in, fold_kv_in, _, _ = others[:5]
        others = others[5:]
    (
        p_context, r_context, tiles, fold_q, lifted, fold_kv, fold_send, fold_reply,
        dk_t, dv_t, raw_q, mixed, keys, values, lows, bias,
    ) = others
    pr = p_context.shape[1]
    rl = r_context.shape[2]
    prompt = bias.shape[1]
    scale = HEAD_DIM ** (-0.5)
    step = scale * LOG2E
    heads = key_a.shape[1] // HEAD_DIM
    wide = query.shape[1] // heads
    share = wide // HEAD_DIM
    block = 512

    me = spot[0]
    places = []
    for other in (0, 1):
        for j in range(8):
            away, far = j // 2, j % 2
            z = jnp.bitwise_xor(me >> 3, far)
            y = jnp.bitwise_and((me >> 1) - away + 4, 3)
            c = jnp.bitwise_xor(jnp.bitwise_and(me, 1), other)
            places.append((other, j, pl.ds(pl.multiple_of((z * 8 + y * 2 + c) * pr, pr), pr)))

    row = lax.broadcasted_iota(jnp.int32, (pr, prompt), 0) + spot[0] * pr
    col = lax.broadcasted_iota(jnp.int32, (pr, prompt), 1)
    bias[...] = jnp.where(col <= row, 0.0, -jnp.inf)
    for other, j, rows in places:
        part = slice(j * pr, (j + 1) * pr)
        lows[rows, :] = (low_a, low_b)[other][part, :]
        for g in range(heads):
            cols = slice(g * HEAD_DIM, (g + 1) * HEAD_DIM)
            keys[g, rows, :] = (key_a, key_b)[other][part, cols]
            values[g, rows, :HEAD_DIM] = (value_a, value_b)[other][part, cols]
    lows[prompt:, :] = r_low[...]
    for g in range(heads):
        cols = slice(g * HEAD_DIM, (g + 1) * HEAD_DIM)
        keys[g, prompt:, :] = r_key[:, cols]
        values[g, prompt:, :HEAD_DIM] = r_value[:, cols]
        values[g, :, HEAD_DIM:] = jnp.ones((prompt + rl, HEAD_DIM), BF16)
    dk_t[...] = jnp.zeros_like(dk_t)
    dv_t[...] = jnp.zeros_like(dv_t)

    def stages(g, n, at, of, mask, keep, cos, sin, count):
        def stack(ref):
            return jnp.concatenate(
                [ref[at : at + n, h * HEAD_DIM : (h + 1) * HEAD_DIM] for h in of], axis=0
            )

        box = {}

        def scores():
            box["q"], box["p"] = stack(query), stack(push)
            box["score"] = mask(mm(box["q"], keys[g, :count, :], NT))

        def softmax():
            score = box.pop("score")
            top = jnp.max(score, axis=1, keepdims=True) * step
            box["weight"] = jnp.exp2(score * step - top).astype(BF16)

        def mix():
            box["summed"] = mm(box["weight"], values[g, :count, :])
            box["dprob"] = mm(box["p"], values[g, :count, :HEAD_DIM], NT)

        def backward():
            summed = box.pop("summed")
            share_of = 1.0 / summed[:, HEAD_DIM:]
            p = box.pop("p").astype(F32)
            context = keep((summed[:, :HEAD_DIM] * share_of).astype(BF16))
            delta = jnp.sum(context.astype(F32) * p, axis=1, keepdims=True)
            box["dscore"] = (box["weight"].astype(F32) * (box.pop("dprob") - delta)).astype(BF16)
            box["inverse"] = share_of * scale
            box["ps"] = (p * share_of).astype(BF16)
            box["qs"] = (box.pop("q").astype(F32) * box["inverse"]).astype(BF16)
            for i, h in enumerate(of):
                part = slice(i * n, (i + 1) * n)
                mixed[at : at + n, h * HEAD_DIM : (h + 1) * HEAD_DIM] = context[part]

        def products():
            dscore = box.pop("dscore")
            dv_t[g, :, :count] += mm(box.pop("ps"), box.pop("weight"), TN)
            dq = mm(dscore, keys[g, :count, :]) * box.pop("inverse")
            dk_t[g, :, :count] += mm(box.pop("qs"), dscore, TN)
            for i, h in enumerate(of):
                part = slice(i * n, (i + 1) * n)
                raw_q[at : at + n, h * HEAD_DIM : (h + 1) * HEAD_DIM] = unrope(
                    dq[part], cos[...], sin[...]
                ).astype(BF16)

        return scores, softmax, mix, backward, products

    p_heads = block // pr
    r_heads = block // rl

    def p_mask(score):
        seen = bias[...]
        return jnp.concatenate(
            [score[i * pr : (i + 1) * pr] + seen for i in range(p_heads)], axis=0
        )

    r_row = lax.broadcasted_iota(jnp.int32, (rl, rl), 0)
    r_col = lax.broadcasted_iota(jnp.int32, (rl, rl), 1)
    r_seen = jnp.concatenate([r_col <= r_row] * r_heads, axis=0)
    live = jnp.concatenate([r_row < lengths[0, 0]] * r_heads, axis=0)

    def r_mask(score):
        own = jnp.where(r_seen, score[:, prompt:], -jnp.inf)
        return jnp.concatenate([score[:, :prompt], own], axis=1)

    def finish(g):
        cols = slice(g * wide, (g + 1) * wide)
        context = mixed[:, cols]
        raw = raw_q[:, cols]
        p_context[0, :, cols] = mixed[:pr, cols]
        r_context[0, 0, :, cols] = mixed[pr:, cols]
        gq = (2.0 * mm(low_t[:RANK, :], raw)).astype(BF16)
        both = mm(lowered_t[...], context)
        god = (2.0 * (both[:RANK] + both[RANK:])).astype(BF16)
        first_tile = g * (2 * share + 2)
        for t in range(share):
            at = slice(t * HEAD_DIM, (t + 1) * HEAD_DIM)
            tiles[first_tile + t] = gq[:, at]
            tiles[first_tile + share + t] = god[:, at]
        upper, lower = dk_t[g, :HALF, :], dk_t[g, HALF:, :]
        cos, sin = cos_t[...], sin_t[...]
        raw_k = jnp.concatenate(
            [(upper * cos + lower * sin).astype(BF16), (lower * cos - upper * sin).astype(BF16)],
            axis=0,
        )
        raw_v = dv_t[g].astype(BF16)
        head = slice(g * HEAD_DIM, (g + 1) * HEAD_DIM)
        gk = jnp.transpose(mm(raw_k, lows[...]))
        gv = jnp.transpose(mm(raw_v, lows[...]))
        tiles[first_tile + 2 * share] = (2.0 * gk[RANK : 2 * RANK]).astype(BF16)
        tiles[first_tile + 2 * share + 1] = (2.0 * gv[2 * RANK : 3 * RANK]).astype(BF16)
        return (
            mm(q_up[:, cols], raw, NT),
            mm(out_down[:, cols], context, NT),
            mm(kv_up[0, :, head], raw_k),
            mm(kv_up[1, :, head], raw_v),
        )

    blocks = []
    for g in range(heads):
        for b in range(share // p_heads):
            of = [g * share + b * p_heads + i for i in range(p_heads)]
            blocks.append(stages(g, pr, 0, of, p_mask, lambda c: c, p_cos, p_sin, prompt))
        for b in range(share // r_heads):
            of = [g * share + b * r_heads + i for i in range(r_heads)]
            blocks.append(
                stages(
                    g, rl, pr, of, r_mask, lambda c: jnp.where(live, c, jnp.zeros_like(c)),
                    r_cos, r_sin, prompt + rl,
                )
            )
    each = len(blocks) // heads
    if first:
        folds = None
    else:
        folds = [fold_q_in[...], lifted_in[...], fold_kv_in[:RANK, :], fold_kv_in[RANK:, :]]
    for at in range(len(blocks) + 1):
        if at < len(blocks):
            blocks[at][0]()
        if at:
            blocks[at - 1][3]()
        if at < len(blocks):
            blocks[at][1]()
        if at:
            blocks[at - 1][4]()
        if at < len(blocks):
            blocks[at][2]()
        if at and at % each == 0:
            new = finish(at // each - 1)
            folds = new if folds is None else [x + y for x, y in zip(folds, new)]
    fold_q[...] = folds[0]
    lifted[...] = folds[1]
    fk, fv = folds[2], folds[3]
    if first:
        fold_kv[:RANK, :] = fk
        fold_kv[RANK:, :] = fv
        return
    for r in range(prompt // pr):
        cols = slice(r * pr, (r + 1) * pr)
        fold_send[r] = jnp.concatenate([fk[:, cols], fv[:, cols]], axis=1).astype(BF16)
    fold_reply[...] = jnp.concatenate([fk[:, prompt:], fv[:, prompt:]], axis=0).astype(BF16)


def grads_kernel(
    spot, fold_q, lifted, fold_reply, fold_recv, p_hidden, r_hidden, p_out, r_out, tiles_a, tiles_b,
    keep, give, held,
):
    pr = p_hidden.shape[1]
    fq = fold_q[...].astype(BF16)
    up = lifted[...].astype(BF16)
    own = jnp.sum(fold_recv[...].astype(F32), axis=0).astype(BF16)
    fp = jnp.concatenate([fq[:, :pr], own[:, :pr], own[:, pr:]], axis=0)
    fr = jnp.concatenate([fq[:, pr:], fold_reply[...]], axis=0)
    wide = p_hidden.shape[2] // HEAD_DIM
    down = (2.0 * (mm(fp, p_hidden[0]) + mm(fr, r_hidden[0, 0]))).astype(BF16)
    grad_up = (2.0 * (mm(up[:, :pr], p_out[0]) + mm(up[:, pr:], r_out[0, 0]))).astype(BF16)
    for t in range(wide):
        cols = slice(t * HEAD_DIM, (t + 1) * HEAD_DIM)
        for j in range(3):
            held[j * wide + t] = down[j * RANK : (j + 1) * RANK, cols]
        held[3 * wide + t] = grad_up[:, cols]
    at = 4 * wide
    small = tiles_a.shape[0]
    held[at : at + small] = tiles_a[...]
    held[at + small : at + 2 * small] = tiles_b[...]
    left = held.shape[0] - at - 2 * small
    held[at + 2 * small :] = jnp.zeros((left, RANK, HEAD_DIM), BF16)
    half = held.shape[0] // 2
    core = jnp.bitwise_and(spot[0], 1)

    @pl.when(core == 0)
    def _():
        keep[...] = held[:half]
        give[...] = held[half:]

    @pl.when(core == 1)
    def _():
        keep[...] = held[half:]
        give[...] = held[:half]


def unpack_kernel(spot, mine, theirs, down, gq, gkv, god, up, held):
    half = mine.shape[0]
    core = jnp.bitwise_and(spot[0], 1)

    @pl.when(core == 0)
    def _():
        held[:half] = mine[...]
        held[half:] = theirs[...]

    @pl.when(core == 1)
    def _():
        held[half:] = mine[...]
        held[:half] = theirs[...]

    def cols(t):
        return slice(t * HEAD_DIM, (t + 1) * HEAD_DIM)

    wide = down.shape[1] // HEAD_DIM
    for t in range(wide):
        for j in range(3):
            down[j * RANK : (j + 1) * RANK, cols(t)] = held[j * wide + t].astype(F32)
        up[:, cols(t)] = held[3 * wide + t].astype(F32)
    at = 4 * wide
    heads = gkv.shape[1] // HEAD_DIM
    share = gq.shape[1] // HEAD_DIM // heads
    for g in range(heads):
        for t in range(share):
            gq[:, cols(g * share + t)] = held[at + t].astype(F32)
            god[:, cols(g * share + t)] = held[at + share + t].astype(F32)
        gkv[:RANK, cols(g)] = held[at + 2 * share].astype(F32)
        gkv[RANK:, cols(g)] = held[at + 2 * share + 1].astype(F32)
        at += 2 * share + 2


def whole(shape):
    return pl.BlockSpec(shape, lambda *_: (0,) * len(shape))


def shifted(x, axis, by):
    n = lax.axis_size(axis)
    return lax.ppermute(x, axis, [(i, (i + by) % n) for i in range(n)])


def chips_of(pair, two):
    one, three = shifted(pair, "y", 1), shifted(pair, "y", 3)
    return [pair, one, two, lax.ppermute(two, "z_lo", PAIR), three]


def per_device(
    prompt_hidden,
    prompt_base,
    reply_hidden,
    reply_base,
    reply_lengths,
    adapter_down,
    query_up_weight,
    key_value_up_weight,
    output_down,
    output_up,
    prompt_grad_out,
    prompt_grad_base,
    reply_grad_out,
    reply_grad_base,
):
    group = lax.axis_size(RESP)
    pr = prompt_hidden.shape[1]
    rl = reply_hidden.shape[2]
    d = prompt_hidden.shape[2]
    prompt = pr * group
    q_width = query_up_weight.shape[1]
    kv_width = key_value_up_weight.shape[2]
    heads = kv_width // HEAD_DIM
    each = heads // 2
    qb = q_width // heads
    share = qb // HEAD_DIM
    rows = pr + rl
    wide = 2 * kv_width + HEAD_DIM
    low_at = 2 * kv_width // HEAD_DIM

    spot = lax.axis_index(RESP).astype(jnp.int32)[None]
    down = jnp.transpose(adapter_down, (0, 2, 1)).reshape(3 * RANK, d)
    out_down = jnp.transpose(output_down)
    cos, sin = rope_tables(prompt + rl)
    cos_rows = jnp.asarray(np.concatenate([cos, cos], axis=1), F32)
    sin_rows = jnp.asarray(np.concatenate([-sin, sin], axis=1), F32)
    cos_t = jnp.asarray(cos.T, F32)
    sin_t = jnp.asarray(sin.T, F32)
    p_table = pl.BlockSpec((pr, HEAD_DIM), lambda i, s: (s[0], 0))
    r_table = pl.BlockSpec((rl, HEAD_DIM), lambda i, *_: (prompt // rl, 0))

    own_kv = pl.pallas_call(
        front_kernel,
        grid_spec=pltpu.PrefetchScalarGridSpec(
            num_scalar_prefetch=1,
            grid=(1,),
            in_specs=[
                whole((1, pr, d)),
                pl.BlockSpec((1, pr, 2 * kv_width), lambda i, s: (0, 0, q_width // (2 * kv_width))),
                whole((3 * RANK, d)),
                whole((2, RANK, kv_width)),
                p_table,
                p_table,
            ],
            out_specs=whole((pr, wide)),
        ),
        out_shape=jax.ShapeDtypeStruct((pr, wide), BF16),
        name="front",
        **params(2 * pr * d * 48, 2_000_000, 56),
    )(spot, prompt_hidden, prompt_base, down, key_value_up_weight, cos_rows, sin_rows)

    far_kv = lax.ppermute(own_kv, "z_lo", PAIR)
    two_kv = shifted(own_kv, "y", 2)

    reply_kv, lows, splits, low_t, lowered_t = pl.pallas_call(
        reply_kernel,
        grid=(1,),
        in_specs=[
            pl.BlockSpec(memory_space=pltpu.SMEM),
            pl.BlockSpec((pr, HEAD_DIM), lambda i: (0, kv_width // HEAD_DIM)),
            whole((1, pr, d)),
            whole((1, 1, rl, d)),
            pl.BlockSpec(
                (1, 1, rl, 2 * kv_width), lambda i: (0, 0, 0, q_width // (2 * kv_width))
            ),
            whole((1, 1, rl, d)),
            whole((3 * RANK, d)),
            whole((2, RANK, kv_width)),
            whole((RANK, d)),
            r_table,
            r_table,
        ],
        out_specs=[
            whole((rl, wide)),
            whole((rows, HEAD_DIM)),
            whole((rows, HEAD_DIM)),
            whole((3 * RANK, rows)),
            whole((2 * RANK, rows)),
        ],
        out_shape=[
            jax.ShapeDtypeStruct((rl, wide), BF16),
            jax.ShapeDtypeStruct((rows, HEAD_DIM), BF16),
            jax.ShapeDtypeStruct((rows, HEAD_DIM), BF16),
            jax.ShapeDtypeStruct((3 * RANK, rows), BF16),
            jax.ShapeDtypeStruct((2 * RANK, rows), BF16),
        ],
        name="reply",
        **params(4 * rows * d * 48, 6_000_000, 56),
    )(
        reply_lengths, own_kv, prompt_grad_out, reply_hidden, reply_base, reply_grad_out, down,
        key_value_up_weight, output_up, cos_rows, sin_rows,
    )

    own_kv, far_kv, two_kv, lows, splits = lax.optimization_barrier(
        (own_kv, far_kv, two_kv, lows, splits)
    )
    cut = kv_width + HEAD_DIM
    parts = chips_of(jnp.concatenate([own_kv, far_kv], axis=0), two_kv)

    def head_cols(n, width, shift=0):
        return pl.BlockSpec((n, width), lambda i, s: (0, i + shift))

    def cols3(shift=0):
        return pl.BlockSpec((1, pr, qb), lambda i, s: (0, 0, i + shift))

    def cols4(shift=0):
        return pl.BlockSpec((1, 1, rl, qb), lambda i, s: (0, 0, 0, i + shift))

    query_a, push_a, query_b, push_b, mark = pl.pallas_call(
        query_kernel,
        grid_spec=pltpu.PrefetchScalarGridSpec(
            num_scalar_prefetch=1,
            grid=(heads,),
            in_specs=[
                pl.BlockSpec(memory_space=pltpu.SMEM),
                whole((rows, HEAD_DIM)),
                whole((rows, HEAD_DIM)),
                cols3(),
                cols3(),
                cols4(),
                cols4(),
                head_cols(RANK, qb),
                head_cols(RANK, qb),
                p_table,
                p_table,
                r_table,
                r_table,
            ],
            out_specs=[
                pl.BlockSpec((rows, qb), lambda i, s: (0, jnp.minimum(i, each - 1))),
                pl.BlockSpec((rows, qb), lambda i, s: (0, jnp.minimum(i, each - 1))),
                pl.BlockSpec((rows, qb), lambda i, s: (0, jnp.maximum(i - each, 0))),
                pl.BlockSpec((rows, qb), lambda i, s: (0, jnp.maximum(i - each, 0))),
                whole((RANK, HEAD_DIM)),
            ],
        ),
        out_shape=[
            jax.ShapeDtypeStruct((rows, q_width // 2), BF16),
            jax.ShapeDtypeStruct((rows, q_width // 2), BF16),
            jax.ShapeDtypeStruct((rows, q_width // 2), BF16),
            jax.ShapeDtypeStruct((rows, q_width // 2), BF16),
            jax.ShapeDtypeStruct((RANK, HEAD_DIM), BF16),
        ],
        name="query",
        **params(4 * rows * q_width * 128, 8_000_000, 48),
    )(
        spot, reply_lengths, lows, splits, prompt_base, prompt_grad_base, reply_base,
        reply_grad_base, query_up_weight, out_down, cos_rows, sin_rows, cos_rows, sin_rows,
    )

    parts, query_a, push_a = lax.optimization_barrier((parts, query_a, push_a))
    first_own = jnp.concatenate([x[:, :cut] for x in parts], axis=0)
    second_own = jnp.concatenate([x[:, cut:] for x in parts], axis=0)
    first_other = lax.ppermute(first_own, "core", PAIR)
    second_other = lax.ppermute(second_own, "core", PAIR)
    count = prompt // 2
    low_block = pl.BlockSpec((count, HEAD_DIM), lambda i, s: (0, kv_width // HEAD_DIM))

    def attend(query, push, own, other, at, before):
        first = before is None
        kb = each * HEAD_DIM
        in_specs = [
            pl.BlockSpec(memory_space=pltpu.SMEM),
            whole((rows, each * qb)),
            whole((rows, each * qb)),
            head_cols(count, kb),
            head_cols(count, kb),
            head_cols(count, kb, 1),
            head_cols(count, kb, 1),
            low_block,
            low_block,
            head_cols(rl, kb, at),
            head_cols(rl, kb, heads // each + at),
            pl.BlockSpec((rl, HEAD_DIM), lambda i, s: (0, low_at)),
            whole((3 * RANK, rows)),
            whole((2 * RANK, rows)),
            head_cols(RANK, each * qb, at),
            pl.BlockSpec((2, RANK, kb), lambda i, s: (0, 0, i + at)),
            head_cols(RANK, each * qb, at),
            p_table,
            p_table,
            r_table,
            r_table,
            whole((HALF, prompt + rl)),
            whole((HALF, prompt + rl)),
        ]
        operands = [
            spot, reply_lengths, query, push, own, other, own, other, first_own, first_other,
            reply_kv, reply_kv, reply_kv, low_t, lowered_t, query_up_weight, key_value_up_weight,
            out_down, cos_rows, sin_rows, cos_rows, sin_rows, cos_t, sin_t,
        ]
        aliases = {}
        if not first:
            aliases = {len(operands) + 3: 0, len(operands) + 4: 1}
            in_specs += [
                whole((RANK, rows)),
                whole((RANK, rows)),
                whole((2 * RANK, prompt + rl)),
                pl.BlockSpec(memory_space=pl.ANY),
                pl.BlockSpec(memory_space=pl.ANY),
            ]
            operands += list(before)
        per_head = 2 * share + 2
        return pl.pallas_call(
            functools.partial(attend_kernel, first),
            grid_spec=pltpu.PrefetchScalarGridSpec(
                num_scalar_prefetch=1,
                grid=(1,),
                in_specs=in_specs,
                out_specs=[
                    pl.BlockSpec((1, pr, each * qb), lambda i, s: (0, 0, i + at)),
                    pl.BlockSpec((1, 1, rl, each * qb), lambda i, s: (0, 0, 0, i + at)),
                    whole((each * per_head, RANK, HEAD_DIM)),
                    whole((RANK, rows)),
                    whole((RANK, rows)),
                    whole((2 * RANK, prompt + rl)),
                    whole((group, RANK, 2 * pr)),
                    whole((2 * RANK, rl)),
                ],
                scratch_shapes=[
                    pltpu.VMEM((each, HEAD_DIM, prompt + rl), F32),
                    pltpu.VMEM((each, HEAD_DIM, prompt + rl), F32),
                    pltpu.VMEM((rows, each * qb), BF16),
                    pltpu.VMEM((rows, each * qb), BF16),
                    pltpu.VMEM((each, prompt + rl, HEAD_DIM), BF16),
                    pltpu.VMEM((each, prompt + rl, 2 * HEAD_DIM), BF16),
                    pltpu.VMEM((prompt + rl, HEAD_DIM), BF16),
                    pltpu.VMEM((pr, prompt), F32),
                ],
            ),
            out_shape=[
                jax.ShapeDtypeStruct((1, pr, q_width), BF16),
                jax.ShapeDtypeStruct((1, 1, rl, q_width), BF16),
                jax.ShapeDtypeStruct((each * per_head, RANK, HEAD_DIM), BF16),
                jax.ShapeDtypeStruct((RANK, rows), F32),
                jax.ShapeDtypeStruct((RANK, rows), F32),
                jax.ShapeDtypeStruct((2 * RANK, prompt + rl), F32),
                jax.ShapeDtypeStruct((group, RANK, 2 * pr), BF16),
                jax.ShapeDtypeStruct((2 * RANK, rl), BF16),
            ],
            input_output_aliases=aliases,
            name="attend",
            **params(12 * rows * prompt * q_width // 2, 8_000_000),
        )(*operands)

    p_half, r_half, tiles_a, fold_q, lifted, fold_kv, _, _ = attend(
        query_a, push_a, first_own, first_other, 0, None
    )
    p_context, r_context, tiles_b, fold_q, lifted, _, fold_send, fold_reply = attend(
        query_b, push_b, second_own, second_other, 1, (fold_q, lifted, fold_kv, p_half, r_half)
    )

    fold_recv = lax.all_to_all(fold_send, RESP, 0, 0, tiled=True)

    slots = 2 * lax.axis_size(CHIPS) * 2
    half = slots // 2
    keep, give = pl.pallas_call(
        grads_kernel,
        grid_spec=pltpu.PrefetchScalarGridSpec(
            num_scalar_prefetch=1,
            grid=(1,),
            in_specs=[
                whole((RANK, rows)),
                whole((RANK, rows)),
                whole((2 * RANK, rl)),
                whole((group, RANK, 2 * pr)),
                whole((1, pr, d)),
                whole((1, 1, rl, d)),
                whole((1, pr, d)),
                whole((1, 1, rl, d)),
                whole(tiles_a.shape),
                whole(tiles_b.shape),
            ],
            out_specs=[whole((half, RANK, HEAD_DIM)), whole((half, RANK, HEAD_DIM))],
            scratch_shapes=[pltpu.VMEM((slots, RANK, HEAD_DIM), BF16)],
        ),
        out_shape=[jax.ShapeDtypeStruct((half, RANK, HEAD_DIM), BF16)] * 2,
        name="grads",
        **params(2 * rows * d * 64, 5_000_000),
    )(
        spot, fold_q, lifted, fold_reply, fold_recv, prompt_hidden, reply_hidden, prompt_grad_out,
        reply_grad_out, tiles_a, tiles_b,
    )

    chips = lax.axis_size(CHIPS)
    got = lax.ppermute(give, "core", PAIR)
    paired = (keep.astype(F32) + got.astype(F32)).astype(BF16)
    spread = lax.all_to_all(
        paired.reshape(chips, -1, HEAD_DIM), CHIPS, 0, 0, tiled=True
    )
    total = jnp.sum(spread.astype(F32), axis=0).astype(BF16)
    mine = lax.all_to_all(
        jnp.broadcast_to(total[None], spread.shape), CHIPS, 0, 0, tiled=True
    ).reshape(half, RANK, HEAD_DIM)
    theirs = lax.ppermute(mine, "core", PAIR)

    shapes = [(3 * RANK, d), (RANK, q_width), (2 * RANK, kv_width), (RANK, q_width), (RANK, d)]
    sum_down, sum_q, sum_kv, sum_od, sum_up = pl.pallas_call(
        unpack_kernel,
        grid_spec=pltpu.PrefetchScalarGridSpec(
            num_scalar_prefetch=1,
            grid=(1,),
            in_specs=[whole((half, RANK, HEAD_DIM))] * 2,
            out_specs=[whole(x) for x in shapes],
            scratch_shapes=[pltpu.VMEM((slots, RANK, HEAD_DIM), BF16)],
        ),
        out_shape=[jax.ShapeDtypeStruct(x, F32) for x in shapes],
        name="unpack",
        **params(0, 3_000_000),
    )(spot, mine, theirs)
    return (
        p_context,
        r_context,
        jnp.transpose(sum_down.reshape(3, RANK, d), (0, 2, 1)),
        sum_q,
        sum_kv.reshape(2, RANK, kv_width),
        jnp.transpose(sum_od),
        sum_up,
    )


def solution(mesh):
    fine = Mesh(mesh.devices.reshape(SIZES), CTX + RESP)
    return jax.shard_map(
        per_device,
        mesh=fine,
        in_specs=(
            P(CTX, RESP, None),
            P(CTX, RESP, None),
            P(CTX, RESP, None, None),
            P(CTX, RESP, None, None),
            P(CTX, RESP),
            P(),
            P(),
            P(),
            P(),
            P(),
            P(CTX, RESP, None),
            P(CTX, RESP, None),
            P(CTX, RESP, None, None),
            P(CTX, RESP, None, None),
        ),
        out_specs=(P(CTX, RESP, None), P(CTX, RESP, None, None), P(), P(), P(), P(), P()),
        check_vma=False,
    )
```
